32 devices in a mesh: seq: 8 (over z, x), grp: 4 (over y, core).
Axes of the slice: x: 2, y: 2, z: 4, core: 2. Of those that a mesh axis runs over, the one named last changes fastest.
Arguments:
- tokens: bfloat16 [4096, 4096], P(('seq', 'grp')), may hold values from -8 to 8
- head_index: int32 [4096, 4], P(('seq', 'grp')), may hold values from 0 to 31, as said below
- gate_fixed: int32 [4096, 4], P(('seq', 'grp')), may hold values from 1 to 32767
- kv_weight: bfloat16 [4096, 4, 256], replicated, may hold values from -0.265625 to 0.265625
- query_weight: bfloat16 [4096, 4096], P('seq', 'grp'), may hold values from -0.265625 to 0.265625
- out_weight: bfloat16 [4096, 4096], P('grp', 'seq'), may hold values from -0.5 to 0.5
Outputs:
- mixed: bfloat16 [4096, 4096], P(('seq', 'grp'))
The draws below stay inside these ranges and needn't reach their ends.
Inputs may be any that keep to these rules, and one draw needn't show every extreme that they name: `head_index`: each row names 4 different head experts lying in exactly 2 of the 4 groups (head e in group e // 8), at least one in each of the two.
All inputs are finite; a program needn't handle non-finite values.
Results may differ from the reference program's by a relative error of at most 0.013.
Values may be sent and summed in bfloat16 or wider, within the bound.
A program may use at most 192 MiB of HBM per device.

```python
import jax
import jax.numpy as jnp
from jax import lax

D = 4096
HD = 128
GROUP_HEADS = 8
TOP = 4
SLOTS = 3
TOK_DEV = 128
SPECIALIST_SETS = 4
HEADS = 32
CAP = 96
STRING_ITEMS = 4096
N_SEQ = 8
N_GRP = 4


def draw_tokens(key, part):
    key = jax.random.fold_in(key, 3)
    first_key = jax.random.fold_in(key, 0)
    values = jnp.clip(jax.random.normal(first_key, (STRING_ITEMS, D), jnp.float32), -6.0, 6.0)
    return values.astype(jnp.bfloat16)


def draw_kv_weight(key, part):
    key = jax.random.fold_in(key, 5)
    values = jnp.clip(jax.random.normal(key, (D, SPECIALIST_SETS, 2 * HD), jnp.float32), -5.0, 5.0) * D ** (-0.5)
    return values.astype(jnp.bfloat16)


def draw_query_weight(key, part):
    key = jax.random.fold_in(key, 6)
    values = jnp.clip(jax.random.normal(key, (D, SPECIALIST_SETS * GROUP_HEADS * HD), jnp.float32), -5.0, 5.0) * D ** (-0.5)
    return values.astype(jnp.bfloat16)


def draw_head_index(key, part):
    key = jax.random.fold_in(key, 7)
    lookup_matrix_lines = jax.random.split(key, 4)
    preference_additive = jax.random.randint(lookup_matrix_lines[0], (SPECIALIST_SETS,), 0, 3) * 12
    cluster_raw_preference = (jax.random.randint(lookup_matrix_lines[1], (STRING_ITEMS, SPECIALIST_SETS), 0, 64) + preference_additive[None, :]) * SPECIALIST_SETS + jnp.arange(SPECIALIST_SETS, dtype=jnp.int32)
    chosen = lax.top_k(cluster_raw_preference, 2)[1].astype(jnp.int32)
    first_count = jax.random.randint(lookup_matrix_lines[2], (STRING_ITEMS, 1), 1, 4)
    head_logit_score = jax.random.randint(lookup_matrix_lines[3], (STRING_ITEMS, 2, GROUP_HEADS), 0, 1024) * GROUP_HEADS + jnp.arange(GROUP_HEADS, dtype=jnp.int32)
    picked = lax.top_k(head_logit_score, 3)[1].astype(jnp.int32)
    column = jnp.broadcast_to(jnp.arange(TOP, dtype=jnp.int32)[None, :], (STRING_ITEMS, TOP))
    in_first = column < first_count
    first_take = jnp.take_along_axis(picked[:, 0, :], jnp.minimum(column, 2), axis=1)
    second_take = jnp.take_along_axis(picked[:, 1, :], jnp.clip(column - first_count, 0, 2), axis=1)
    local_head = jnp.where(in_first, first_take, second_take)
    group = jnp.where(in_first, chosen[:, 0:1], chosen[:, 1:2])
    return (group * GROUP_HEADS + local_head).astype(jnp.int32)


def with_ends(drawn, rng, least, high):
    shape = drawn.shape
    place = [jax.random.randint(jax.random.fold_in(rng, axis), (), 0, shape[axis]) for axis in range(len(shape))]
    drawn = drawn.at[tuple(place)].set(least)
    longest = shape.index(max(shape))
    place[longest] = (place[longest] + 1) % shape[longest]
    return drawn.at[tuple(place)].set(high)


def levels(key, dims, cuts, smallest, largest):
    gain, own = 1.0, jax.random.fold_in(key, 6)
    for axis_at, parts in cuts:
        draws = jnp.exp(jax.random.uniform(jax.random.fold_in(own, axis_at), (parts,), jnp.float32, smallest / len(cuts), largest / len(cuts)))
        gain = gain * jnp.repeat(draws, dims[axis_at] // parts).reshape([-1 if axis == axis_at else 1 for axis in range(len(dims))])
    return gain


def centred(own_key, extent, width, reach, cuts=(), kind=jnp.bfloat16):
    entries = width * jax.random.normal(own_key, extent, jnp.float32)
    if cuts:
        entries = entries * levels(own_key, extent, cuts, -0.22, 0.18)
    return jnp.clip(entries, -reach, reach).astype(kind)


def setup_inputs(seed: int = 0) -> dict:
    keys = jax.random.split(jax.random.key(seed), 7)
    return {
        "tokens": draw_tokens(jax.random.fold_in(keys[6], 71), 0),
        "head_index": draw_head_index(jax.random.fold_in(keys[6], 71), 0),
        "gate_fixed": with_ends(jax.random.randint(keys[2], (STRING_ITEMS, TOP), 1, 32768), jax.random.fold_in(keys[2], 1), 1, 32767).astype(jnp.int32),
        "kv_weight": draw_kv_weight(jax.random.fold_in(keys[6], 71), 0),
        "query_weight": draw_query_weight(jax.random.fold_in(keys[6], 71), 0),
        "out_weight": centred(keys[5], (HEADS * HD, D), HD ** -0.5, 0.5, ((0, 4), (1, 8))),
    }


def route_tables(head_index, gate_fixed):
    count_rows = head_index.shape[0]
    cluster_membership = head_index // GROUP_HEADS
    local_head = head_index % GROUP_HEADS
    in_group = cluster_membership[:, None, :] == jnp.arange(SPECIALIST_SETS, dtype=jnp.int32)[None, :, None]
    slot_order = jnp.cumsum(in_group.astype(jnp.int32), axis=2) - 1
    picked = (in_group[:, :, :, None] & (slot_order[:, :, :, None] == jnp.arange(SLOTS, dtype=jnp.int32))).astype(jnp.int32)
    slot_head = jnp.sum(picked * local_head[:, None, :, None], axis=2)
    slot_gate = jnp.sum(picked * gate_fixed[:, None, :, None], axis=2)
    member = jnp.any(in_group, axis=2).astype(jnp.int32)
    ranking = (jnp.cumsum(member.reshape(count_rows // TOK_DEV, TOK_DEV, SPECIALIST_SETS), axis=1) - 1).reshape(count_rows, SPECIALIST_SETS)
    retained = (member > 0) & (ranking < CAP)
    selected = (retained[:, :, None] & (ranking[:, :, None] == jnp.arange(CAP, dtype=jnp.int32))).astype(jnp.int32)
    return selected, slot_head, slot_gate


def reference(tokens, head_index, gate_fixed, kv_weight, query_weight, out_weight):
    shard_rows = N_GRP * TOK_DEV
    slot_rows = N_GRP * CAP
    kv_all = jnp.dot(tokens, kv_weight.reshape(D, SPECIALIST_SETS * 2 * HD), preferred_element_type=jnp.float32)
    kv_all = kv_all.astype(jnp.bfloat16).reshape(STRING_ITEMS, SPECIALIST_SETS, 2 * HD)
    selected, slot_head, slot_gate = route_tables(head_index, gate_fixed)
    positions = jnp.arange(STRING_ITEMS, dtype=jnp.int32)
    score_scale = HD ** -0.5
    query_groups = query_weight.reshape(D, SPECIALIST_SETS, GROUP_HEADS * HD)
    out_groups = out_weight.reshape(SPECIALIST_SETS, GROUP_HEADS * HD, D)
    identity = jnp.eye(N_GRP, dtype=jnp.int32)
    pieces = []
    for shard in range(N_SEQ):
        lower = shard * shard_rows
        upper = lower + shard_rows
        x_part = tokens[lower:upper]
        selection_portion = selected[lower:upper].reshape(N_GRP, TOK_DEV, SPECIALIST_SETS, CAP)
        kv_part = kv_all[:upper]
        key_pos = jnp.arange(upper, dtype=jnp.int32)
        pos_part = positions[lower:upper]
        head_part = slot_head[lower:upper]
        gate_part = slot_gate[lower:upper]

        def one_group(group):
            blocks = jnp.transpose(selection_portion[:, :, group, :], (0, 2, 1))
            matrix = (blocks[:, :, None, :] * identity[:, None, :, None]).reshape(slot_rows, shard_rows)
            place_entries = jnp.dot(matrix.astype(jnp.bfloat16), x_part, preferred_element_type=jnp.float32).astype(jnp.bfloat16)
            slot_pos = jnp.sum(matrix * pos_part[None, :], axis=1)
            heads = jnp.sum(matrix[:, :, None] * head_part[:, group, :][None, :, :], axis=1)
            gates = jnp.sum(matrix[:, :, None] * gate_part[:, group, :][None, :, :], axis=1).astype(jnp.float32) / 32768.0
            q_all = jnp.dot(place_entries, query_groups[:, group, :], preferred_element_type=jnp.float32)
            q_all = q_all.reshape(slot_rows, GROUP_HEADS, HD)
            indicator_vector = (heads[:, :, None] == jnp.arange(GROUP_HEADS, dtype=jnp.int32)).astype(jnp.float32)
            queries = jnp.einsum("rjh,rhd->rjd", indicator_vector, q_all, precision=lax.Precision.HIGHEST)
            queries = queries.astype(jnp.bfloat16).reshape(slot_rows * SLOTS, HD)
            query_pos = jnp.repeat(slot_pos, SLOTS)
            lookup_matrix_lines = kv_part[:, group, :HD]
            values = kv_part[:, group, HD:]
            scores = jnp.dot(queries, lookup_matrix_lines.T, preferred_element_type=jnp.float32) * score_scale
            visible = key_pos[None, :] <= query_pos[:, None]
            scores = jnp.where(visible, scores, -jnp.inf)
            highest = jnp.max(scores, axis=1, keepdims=True)
            weights = jnp.exp(scores - highest)
            total = jnp.sum(weights, axis=1)
            head_out = jnp.dot(weights.astype(jnp.bfloat16), values, preferred_element_type=jnp.float32) / total[:, None]
            gated = head_out.reshape(slot_rows, SLOTS, HD) * gates[:, :, None]
            weighted = jnp.einsum("rjh,rjd->rhd", indicator_vector, gated, precision=lax.Precision.HIGHEST)
            weighted = weighted.astype(jnp.bfloat16).reshape(slot_rows, GROUP_HEADS * HD)
            head_contribution = jnp.dot(weighted, out_groups[group], preferred_element_type=jnp.float32).astype(jnp.bfloat16)
            return jnp.dot(matrix.T.astype(jnp.bfloat16), head_contribution, preferred_element_type=jnp.float32)

        partial_sums = lax.map(one_group, jnp.arange(SPECIALIST_SETS, dtype=jnp.int32))
        pieces.append(jnp.sum(partial_sums, axis=0).astype(jnp.bfloat16))
    return jnp.concatenate(pieces, axis=0)
```

```python
import functools

import jax
import jax.numpy as jnp
from jax import lax
from jax.experimental import pallas as pl
from jax.experimental.pallas import tpu as pltpu
from jax.sharding import PartitionSpec as P


def route_tables(head_index, gate_fixed, groups, capacity, group_heads):
    slots = head_index.shape[1] - 1
    cluster_membership = head_index // group_heads
    local_head = head_index % group_heads
    in_group = cluster_membership[:, None, :] == jnp.arange(groups, dtype=jnp.int32)[None, :, None]
    slot_order = jnp.cumsum(in_group.astype(jnp.int32), axis=2) - 1
    picked = (
        in_group[:, :, :, None] & (slot_order[:, :, :, None] == jnp.arange(slots, dtype=jnp.int32))
    ).astype(jnp.int32)
    slot_head = jnp.sum(picked * local_head[:, None, :, None], axis=2)
    slot_gate = jnp.sum(picked * gate_fixed[:, None, :, None], axis=2)
    member = jnp.any(in_group, axis=2).astype(jnp.int32)
    ranking = jnp.cumsum(member, axis=0) - 1
    retained = (member > 0) & (ranking < capacity)
    selected = (
        retained[:, :, None] & (ranking[:, :, None] == jnp.arange(capacity, dtype=jnp.int32))
    ).astype(jnp.int32)
    return (selected, slot_head, slot_gate)


MESH = pl.DeviceIdType.MESH
KV, WQ, WO = 0, 1, 2


def kernel(
    nz, nx, ng, group_heads, slots,
    rows_in, kv_in, wq_in, wo_in, heads_ref, gates_ref, pos_ref, sel_ref,
    out_ref,
    rows, kvs, wq, wo, q_all, queries, acc, top, total, weighted, contrib, back,
    local_sem, row_send, row_recv, kv_send, kv_recv, gather_send, gather_recv, back_send, back_recv,
):
    nb = nz * nx
    s, g = lax.axis_index("seq"), lax.axis_index("grp")
    z, x = s // nx, s % nx
    _, cap, width = rows.shape
    slot_rows = ng * cap
    depth = wq.shape[1]
    out_cols = wo.shape[2]
    tok = kvs.shape[2]
    keys = ng * tok
    hd = kvs.shape[3] // 2
    bufs = (kvs, wq, wo)

    def xs(k):
        return (z * nx + (x + k) % nx, g)

    def peer(k):
        return (g + k) % ng

    barrier = pltpu.get_barrier_semaphore()

    def greet(dev):
        pl.semaphore_signal(barrier, inc=1, device_id=dev, device_id_type=MESH)

    for k in range(1, nx):
        greet(xs(k))
    for k in range(1, ng):
        greet((s, peer(k)))

    @pl.when(z > 0)
    def _():
        greet((s - nx, g))

    @pl.when(z < nz - 1)
    def _():
        greet((s + nx, g))

    peers = nx - 1 + ng - 1 + (z > 0).astype(jnp.int32) + (z < nz - 1).astype(jnp.int32)
    pl.semaphore_wait(barrier, peers)

    own = [
        pltpu.make_async_copy(wq_in, wq.at[s], local_sem.at[0]),
        pltpu.make_async_copy(kv_in.at[g], kvs.at[s, g], local_sem.at[1]),
        pltpu.make_async_copy(rows_in.at[g], rows.at[g], local_sem.at[2]),
        pltpu.make_async_copy(wo_in, wo.at[s], local_sem.at[3]),
    ]
    for copy in own:
        copy.start()

    def kv_copy(k):
        to = peer(k)
        return pltpu.make_async_remote_copy(
            kv_in.at[to], kvs.at[s, g], kv_send.at[k - 1], kv_recv.at[k - 1], (s, to), MESH
        )

    def kv_arrival(k):
        frm = peer(ng - k)
        return pltpu.make_async_remote_copy(
            kv_in.at[g], kvs.at[s, frm], kv_send.at[k - 1], kv_recv.at[k - 1], (s, frm), MESH
        )

    def row_copy(k):
        to = peer(k)
        return pltpu.make_async_remote_copy(
            rows_in.at[to], rows.at[g], row_send.at[k - 1], row_recv.at[k - 1], (s, to), MESH
        )

    def row_arrival(k):
        frm = peer(ng - k)
        return pltpu.make_async_remote_copy(
            rows_in.at[g], rows.at[frm], row_send.at[k - 1], row_recv.at[k - 1], (s, frm), MESH
        )

    def gather(t, zz, kind, dev):
        b = zz * nx + x
        return pltpu.make_async_remote_copy(
            bufs[t].at[b], bufs[t].at[b],
            gather_send.at[(t * nz + zz) * (nx + 1) + kind],
            gather_recv.at[t * nb + b], dev, MESH,
        )

    def arrival(t, b):
        return pltpu.make_async_remote_copy(
            bufs[t].at[b], bufs[t].at[b], gather_send.at[0], gather_recv.at[t * nb + b],
            (s, peer(1)), MESH,
        )

    def across(t, zz):
        for k in range(1, nx):
            gather(t, zz, 1 + k, xs(k)).start()

    def up(t, zz):
        @pl.when(z < nz - 1)
        def _():
            gather(t, zz, 0, (s + nx, g)).start()

    def down(t, zz):
        @pl.when(z > 0)
        def _():
            gather(t, zz, 1, (s - nx, g)).start()

    def send_own(t):
        up(t, z)
        down(t, z)
        across(t, z)

    def stage(t, d):
        @pl.when(z - d >= 0)
        def _():
            arrival(t, (z - d) * nx + x).wait_recv()
            up(t, z - d)
            across(t, z - d)

        @pl.when(z + d < nz)
        def _():
            arrival(t, (z + d) * nx + x).wait_recv()
            down(t, z + d)
            across(t, z + d)

    for k in range(1, ng):
        kv_copy(k).start()
    own[0].wait()
    send_own(WQ)
    for k in range(1, ng):
        row_copy(k).start()
    own[1].wait()
    for k in range(1, ng):
        kv_arrival(k).wait_recv()
    send_own(KV)
    own[2].wait()
    own[3].wait()
    for d in range(1, nz):
        stage(KV, d)
        stage(WQ, d)
    send_own(WO)

    for k in range(1, ng):
        row_arrival(k).wait_recv()

    def block_at(i):
        flip = jnp.where(z * 2 < nz, i % nz, nz - 1 - i % nz)
        return flip * nx + (x + i // nz) % nx

    q_all[...] = jnp.zeros_like(q_all)

    def project(i, carry):
        b = block_at(i)

        @pl.when(i >= nz)
        def _():
            arrival(WQ, b).wait_recv()

        piece = rows[:, :, pl.ds(pl.multiple_of(b * depth, 128), depth)].reshape(slot_rows, depth)
        q_all[...] += jnp.dot(piece, wq[b], preferred_element_type=jnp.float32)
        return carry

    lax.fori_loop(0, nb, project, 0)

    for j in range(slots):
        head = heads_ref[:, j : j + 1]
        q = jnp.zeros((slot_rows, hd), jnp.float32)
        for h in range(group_heads):
            q = jnp.where(head == h, q_all[:, h * hd : (h + 1) * hd], q)
        queries[j] = q.astype(jnp.bfloat16)

    for i in range(nz, nb):
        arrival(KV, block_at(i)).wait_recv()

    def update(j, b, masked):
        k = kvs[b, :, :, :hd].reshape(keys, hd)
        v = kvs[b, :, :, hd:].reshape(keys, hd)
        scores = lax.dot_general(
            queries[j], k, (((1,), (1,)), ((), ())), preferred_element_type=jnp.float32
        ) * (hd ** -0.5)
        if masked:
            key_pos = b * keys + lax.broadcasted_iota(jnp.int32, scores.shape, 1)
            scores = jnp.where(key_pos <= pos_ref[...], scores, -1e30)
        before = top[...]
        newest = jnp.maximum(before, jnp.max(scores, axis=1, keepdims=True))
        weights = jnp.exp(scores - newest)
        factor = jnp.exp(before - newest)
        total[...] = total[...] * factor + jnp.sum(weights, axis=1, keepdims=True)
        acc[j] = acc[j] * factor + jnp.dot(
            weights.astype(jnp.bfloat16), v, preferred_element_type=jnp.float32
        )
        top[...] = newest

    def attend(j):
        top[...] = jnp.full_like(top, -1e30)
        total[...] = jnp.zeros_like(total)
        acc[j] = jnp.zeros((slot_rows, hd), jnp.float32)

        def step(b, carry):
            update(j, b, False)
            return carry

        lax.fori_loop(0, s, step, 0)
        update(j, s, True)
        acc[j] = acc[j] / total[...] * gates_ref[:, j : j + 1]

    for n in range(max(nz - 1, slots)):
        if n < slots:
            attend(n)
        if n < nz - 1:
            stage(WO, n + 1)

    for h in range(group_heads):
        value = jnp.zeros((slot_rows, hd), jnp.float32)
        for j in range(slots):
            value += jnp.where(heads_ref[:, j : j + 1] == h, acc[j], 0.0)
        weighted[:, h * hd : (h + 1) * hd] = value.astype(jnp.bfloat16)

    def back_copy(b, k):
        to = peer(k)
        return pltpu.make_async_remote_copy(
            contrib.at[b, to], back.at[b, g],
            back_send.at[b * (ng - 1) + k - 1], back_recv.at[b * (ng - 1) + k - 1], (s, to), MESH,
        )

    def back_arrival(b, k):
        frm = peer(ng - k)
        return pltpu.make_async_remote_copy(
            contrib.at[b, g], back.at[b, frm],
            back_send.at[b * (ng - 1) + k - 1], back_recv.at[b * (ng - 1) + k - 1], (s, frm), MESH,
        )

    def give_back(i, carry):
        b = block_at(i)

        @pl.when(i >= nz)
        def _():
            arrival(WO, b).wait_recv()

        product = jnp.dot(weighted[...], wo[b], preferred_element_type=jnp.float32)
        contrib[b] = product.astype(jnp.bfloat16).reshape(ng, cap, out_cols)
        for k in range(1, ng):
            back_copy(b, k).start()
        back[b, g] = contrib[b, g]
        return carry

    lax.fori_loop(0, nb, give_back, 0)

    def combine(i, carry):
        b = block_at(i)
        for k in range(1, ng):
            back_arrival(b, k).wait_recv()
        mixed = jnp.dot(
            sel_ref[...], back[b].reshape(slot_rows, out_cols), preferred_element_type=jnp.float32
        )
        out_ref[:, pl.ds(pl.multiple_of(b * out_cols, 128), out_cols)] = mixed.astype(jnp.bfloat16)
        for k in range(1, ng):
            back_copy(b, k).wait_send()
        return carry

    lax.fori_loop(0, nb, combine, 0)

    for k in range(1, ng):
        kv_copy(k).wait_send()
        row_copy(k).wait_send()
    for t in (KV, WQ, WO):
        for zz in range(nz):
            @pl.when((zz <= z) & (z < nz - 1))
            def _():
                gather(t, zz, 0, (s + nx, g)).wait_send()

            @pl.when((zz >= z) & (z > 0))
            def _():
                gather(t, zz, 1, (s - nx, g)).wait_send()

            for k in range(1, nx):
                gather(t, zz, 1 + k, xs(k)).wait_send()


def on_device(nz, tokens, head_index, gate_fixed, kv_weight, query_weight, out_weight):
    groups = lax.axis_size("grp")
    nb = lax.axis_size("seq")
    nx = nb // nz
    tok_rows, model_width = tokens.shape
    capacity = 3 * tok_rows // groups
    head_width = kv_weight.shape[2] // 2
    group_heads = query_weight.shape[1] // head_width
    slots = head_index.shape[1] - 1
    offset = (lax.axis_index("seq") * groups + lax.axis_index("grp")) * tok_rows
    positions = offset + jnp.arange(tok_rows, dtype=jnp.int32)
    kv_local = jnp.einsum(
        "td,dgc->gtc", tokens, kv_weight, preferred_element_type=jnp.float32
    ).astype(jnp.bfloat16)
    selected, slot_head, slot_gate = route_tables(
        head_index, gate_fixed, groups, capacity, group_heads
    )
    by_slot = jnp.transpose(selected, (1, 2, 0))
    by_slot_bf = by_slot.astype(jnp.bfloat16)
    send_tokens = jnp.einsum(
        "gct,td->gcd", by_slot_bf, tokens, preferred_element_type=jnp.float32
    ).astype(jnp.bfloat16)
    send_pos = jnp.sum(by_slot * positions[None, None, :], axis=2)
    send_head = jnp.sum(
        by_slot[:, :, :, None] * jnp.transpose(slot_head, (1, 0, 2))[:, None, :, :], axis=2
    )
    send_gate = jnp.sum(
        by_slot[:, :, :, None] * jnp.transpose(slot_gate, (1, 0, 2))[:, None, :, :], axis=2
    )
    send_meta = jnp.concatenate([send_head, send_gate, send_pos[:, :, None]], axis=2)
    recv_meta = lax.all_to_all(send_meta, "grp", split_axis=0, concat_axis=0, tiled=True)
    slot_rows = groups * capacity
    recv_meta = recv_meta.reshape(slot_rows, 2 * slots + 1)
    heads = recv_meta[:, :slots]
    gates = recv_meta[:, slots : 2 * slots].astype(jnp.float32) / 32768.0
    slot_pos = recv_meta[:, 2 * slots :]
    sel = by_slot_bf.reshape(slot_rows, tok_rows).T
    bf, f32 = jnp.bfloat16, jnp.float32
    depth, q_cols = query_weight.shape
    out_cols = out_weight.shape[1]
    any_spec = pl.BlockSpec(memory_space=pl.ANY)
    vmem_spec = pl.BlockSpec(memory_space=pltpu.VMEM)
    dma = pltpu.SemaphoreType.DMA
    return pl.pallas_call(
        functools.partial(kernel, nz, nx, groups, group_heads, slots),
        out_shape=jax.ShapeDtypeStruct((tok_rows, model_width), bf),
        in_specs=[any_spec] * 4 + [vmem_spec] * 4,
        out_specs=vmem_spec,
        scratch_shapes=[
            pltpu.VMEM((groups, capacity, model_width), bf),
            pltpu.VMEM((nb, groups, tok_rows, 2 * head_width), bf),
            pltpu.VMEM((nb, depth, q_cols), bf),
            pltpu.VMEM((nb, q_cols, out_cols), bf),
            pltpu.VMEM((slot_rows, q_cols), f32),
            pltpu.VMEM((slots, slot_rows, head_width), bf),
            pltpu.VMEM((slots, slot_rows, head_width), f32),
            pltpu.VMEM((slot_rows, 1), f32),
            pltpu.VMEM((slot_rows, 1), f32),
            pltpu.VMEM((slot_rows, q_cols), bf),
            pltpu.VMEM((nb, groups, capacity, out_cols), bf),
            pltpu.VMEM((nb, groups, capacity, out_cols), bf),
            dma((4,)),
            dma((groups - 1,)),
            dma((groups - 1,)),
            dma((groups - 1,)),
            dma((groups - 1,)),
            dma((3 * nz * (nx + 1),)),
            dma((3 * nb,)),
            dma((nb * (groups - 1),)),
            dma((nb * (groups - 1),)),
        ],
        compiler_params=pltpu.CompilerParams(
            collective_id=0, has_side_effects=True, vmem_limit_bytes=56 * 2**20
        ),
    )(send_tokens, kv_local, query_weight, out_weight, heads, gates, slot_pos, sel)


def solution(mesh):
    in_specs = (
        P(("seq", "grp"), None),
        P(("seq", "grp"), None),
        P(("seq", "grp"), None),
        P(),
        P("seq", "grp"),
        P("grp", "seq"),
    )
    out_specs = P(("seq", "grp"), None)
    nz = 4 if mesh.shape["seq"] % 4 == 0 else 1
    return jax.shard_map(
        functools.partial(on_device, nz),
        mesh=mesh, in_specs=in_specs, out_specs=out_specs, check_vma=False,
    )
```

```python
import functools

import jax
import jax.numpy as jnp
from jax import lax
from jax.experimental import pallas as pl
from jax.experimental.pallas import tpu as pltpu
from jax.sharding import PartitionSpec as P


def route_tables(head_index, gate_fixed, groups, capacity, group_heads):
    slots = head_index.shape[1] - 1
    cluster_membership = head_index // group_heads
    local_head = head_index % group_heads
    in_group = cluster_membership[:, None, :] == jnp.arange(groups, dtype=jnp.int32)[None, :, None]
    slot_order = jnp.cumsum(in_group.astype(jnp.int32), axis=2) - 1
    picked = (
        in_group[:, :, :, None] & (slot_order[:, :, :, None] == jnp.arange(slots, dtype=jnp.int32))
    ).astype(jnp.int32)
    slot_head = jnp.sum(picked * local_head[:, None, :, None], axis=2)
    slot_gate = jnp.sum(picked * gate_fixed[:, None, :, None], axis=2)
    member = jnp.any(in_group, axis=2).astype(jnp.int32)
    ranking = jnp.cumsum(member, axis=0) - 1
    retained = (member > 0) & (ranking < capacity)
    selected = (
        retained[:, :, None] & (ranking[:, :, None] == jnp.arange(capacity, dtype=jnp.int32))
    ).astype(jnp.int32)
    return (selected, slot_head, slot_gate)


MESH = pl.DeviceIdType.MESH
KV, WQ, WO = 0, 1, 2


def kernel(
    nz, nx, ng, group_heads, slots,
    rows_in, kv_in, wq_in, wo_in, heads_ref, gates_ref, pos_ref, sel_ref,
    out_ref,
    rows, kvs, wq, wo, q_all, queries, acc, top, total, weighted, contrib, back,
    local_sem, row_send, row_recv, kv_send, kv_recv, gather_send, gather_recv, back_send, back_recv,
    half_send, half_recv,
):
    nb = nz * nx
    s, g = lax.axis_index("seq"), lax.axis_index("grp")
    z, x = s // nx, s % nx
    _, cap, width = rows.shape
    slot_rows = ng * cap
    depth = wq.shape[1]
    out_cols = wo.shape[2]
    tok = kvs.shape[2]
    keys = ng * tok
    hd = kvs.shape[3] // 2
    bufs = (kvs, wq, wo)

    def xs(k):
        return (z * nx + (x + k) % nx, g)

    def peer(k):
        return (g + k) % ng

    barrier = pltpu.get_barrier_semaphore()

    def greet(dev):
        pl.semaphore_signal(barrier, inc=1, device_id=dev, device_id_type=MESH)

    for k in range(1, nx):
        greet(xs(k))
    for k in range(1, ng):
        greet((s, peer(k)))

    @pl.when(z > 0)
    def _():
        greet((s - nx, g))

    @pl.when(z < nz - 1)
    def _():
        greet((s + nx, g))

    peers = nx - 1 + ng - 1 + (z > 0).astype(jnp.int32) + (z < nz - 1).astype(jnp.int32)
    pl.semaphore_wait(barrier, peers)

    own = [
        pltpu.make_async_copy(wq_in, wq.at[s], local_sem.at[0]),
        pltpu.make_async_copy(kv_in.at[g], kvs.at[s, g], local_sem.at[1]),
        pltpu.make_async_copy(rows_in.at[g], rows.at[g], local_sem.at[2]),
        pltpu.make_async_copy(wo_in, wo.at[s], local_sem.at[3]),
    ]
    for copy in own:
        copy.start()

    def kv_copy(k):
        to = peer(k)
        return pltpu.make_async_remote_copy(
            kv_in.at[to], kvs.at[s, g], kv_send.at[k - 1], kv_recv.at[k - 1], (s, to), MESH
        )

    def kv_arrival(k):
        frm = peer(ng - k)
        return pltpu.make_async_remote_copy(
            kv_in.at[g], kvs.at[s, frm], kv_send.at[k - 1], kv_recv.at[k - 1], (s, frm), MESH
        )

    def row_copy(k):
        to = peer(k)
        return pltpu.make_async_remote_copy(
            rows_in.at[to], rows.at[g], row_send.at[k - 1], row_recv.at[k - 1], (s, to), MESH
        )

    def row_arrival(k):
        frm = peer(ng - k)
        return pltpu.make_async_remote_copy(
            rows_in.at[g], rows.at[frm], row_send.at[k - 1], row_recv.at[k - 1], (s, frm), MESH
        )

    def part(t, b, which):
        if which is None:
            return bufs[t].at[b]
        rows_half = bufs[t].shape[1] // 2
        return bufs[t].at[b, which * rows_half : (which + 1) * rows_half]

    def is_end(zz):
        return (zz == 0) | (zz == nz - 1)

    def gather(t, zz, kind, dev, which=None):
        here = part(t, zz * nx + x, which)
        return pltpu.make_async_remote_copy(
            here, here,
            gather_send.at[(t * nz + zz) * (nx + 1) + kind],
            gather_recv.at[t * nb + zz * nx + x], dev, MESH,
        )

    def arrival(t, b, which=None):
        here = part(t, b, which)
        return pltpu.make_async_remote_copy(
            here, here, gather_send.at[0], gather_recv.at[t * nb + b], (s, peer(1)), MESH
        )

    def half(t, way, k):
        end = 0 if way == 0 else nz - 1
        here = part(t, end * nx + (x + k) % nx, 1)
        at = (t * 2 + way) * nx + k
        to = s + nx if way == 0 else s - nx
        return pltpu.make_async_remote_copy(
            here, here, half_send.at[at], half_recv.at[at], (to, g), MESH
        )

    def half_arrival(t, way, k):
        end = 0 if way == 0 else nz - 1
        here = part(t, end * nx + (x + k) % nx, 1)
        at = (t * 2 + way) * nx + k
        return pltpu.make_async_remote_copy(
            here, here, half_send.at[at], half_recv.at[at], (s, peer(1)), MESH
        )

    def up(t, zz):
        @pl.when(z < nz - 1)
        def _():
            gather(t, zz, 0, (s + nx, g)).start()

    def down(t, zz):
        @pl.when(z > 0)
        def _():
            gather(t, zz, 1, (s - nx, g)).start()

    def send_own(t):
        up(t, z)
        down(t, z)
        for k in range(1, nx):
            gather(t, z, 1 + k, xs(k)).start()

    def across(t, zz):
        @pl.when(is_end(zz))
        def _():
            for k in range(1, nx):
                gather(t, zz, 1 + k, xs(k), 0).start()

        @pl.when(jnp.logical_not(is_end(zz)))
        def _():
            for k in range(1, nx):
                gather(t, zz, 1 + k, xs(k)).start()

    def column_stage(t, d):
        @pl.when(z - d >= 0)
        def _():
            arrival(t, (z - d) * nx + x).wait_recv()
            up(t, z - d)
            across(t, z - d)

        @pl.when(z + d < nz)
        def _():
            arrival(t, (z + d) * nx + x).wait_recv()
            down(t, z + d)
            across(t, z + d)

    def half_stage(t, e):
        for way in (0, 1):
            @pl.when(z == (e if way == 0 else nz - 1 - e))
            def _():
                for k in range(1, nx):
                    if e == 0:
                        arrival(t, z * nx + (x + k) % nx).wait_recv()
                    else:
                        half_arrival(t, way, k).wait_recv()
                    half(t, way, k).start()

    def stage(t, d):
        column_stage(t, d)
        if d == 1:
            half_stage(t, 0)
        if d < nz - 1:
            half_stage(t, d)

    def consume(t, zz, k):
        b = zz * nx + (x + k) % nx

        @pl.when((zz == z) & jnp.logical_not(is_end(z)))
        def _():
            arrival(t, b).wait_recv()

        @pl.when((zz != z) & jnp.logical_not(is_end(zz)))
        def _():
            arrival(t, b).wait_recv()

        @pl.when((zz != z) & is_end(zz))
        def _():
            arrival(t, b, 0).wait_recv()

        @pl.when((zz == 0) & (z == nz - 1))
        def _():
            half_arrival(t, 0, k).wait_recv()

        @pl.when((zz == nz - 1) & (z == 0))
        def _():
            half_arrival(t, 1, k).wait_recv()

    for k in range(1, ng):
        kv_copy(k).start()
    own[0].wait()
    send_own(WQ)
    for k in range(1, ng):
        row_copy(k).start()
    own[1].wait()
    for k in range(1, ng):
        kv_arrival(k).wait_recv()
    send_own(KV)
    own[2].wait()
    own[3].wait()
    for d in range(1, nz):
        stage(KV, d)
        stage(WQ, d)
    send_own(WO)

    for k in range(1, ng):
        row_arrival(k).wait_recv()

    def shard_at(i):
        return jnp.where(z * 2 < nz, i % nz, nz - 1 - i % nz)

    def block_at(i):
        return shard_at(i) * nx + (x + i // nz) % nx

    def consume_from(t, i):
        for k in range(1, nx):
            @pl.when(i // nz == k)
            def _():
                consume(t, shard_at(i), k)

    q_all[...] = jnp.zeros_like(q_all)

    def project(i, carry):
        b = block_at(i)

        consume_from(WQ, i)

        piece = rows[:, :, pl.ds(pl.multiple_of(b * depth, 128), depth)].reshape(slot_rows, depth)
        q_all[...] += jnp.dot(piece, wq[b], preferred_element_type=jnp.float32)
        return carry

    lax.fori_loop(0, nb, project, 0)

    for j in range(slots):
        head = heads_ref[:, j : j + 1]
        q = jnp.zeros((slot_rows, hd), jnp.float32)
        for h in range(group_heads):
            q = jnp.where(head == h, q_all[:, h * hd : (h + 1) * hd], q)
        queries[j] = q.astype(jnp.bfloat16)

    for k in range(1, nx):
        for zz in range(nz):
            consume(KV, zz, k)

    def update(j, b, masked):
        k = kvs[b, :, :, :hd].reshape(keys, hd)
        v = kvs[b, :, :, hd:].reshape(keys, hd)
        scores = lax.dot_general(
            queries[j], k, (((1,), (1,)), ((), ())), preferred_element_type=jnp.float32
        ) * (hd ** -0.5)
        if masked:
            key_pos = b * keys + lax.broadcasted_iota(jnp.int32, scores.shape, 1)
            scores = jnp.where(key_pos <= pos_ref[...], scores, -1e30)
        before = top[...]
        newest = jnp.maximum(before, jnp.max(scores, axis=1, keepdims=True))
        weights = jnp.exp(scores - newest)
        factor = jnp.exp(before - newest)
        total[...] = total[...] * factor + jnp.sum(weights, axis=1, keepdims=True)
        acc[j] = acc[j] * factor + jnp.dot(
            weights.astype(jnp.bfloat16), v, preferred_element_type=jnp.float32
        )
        top[...] = newest

    def attend(j):
        top[...] = jnp.full_like(top, -1e30)
        total[...] = jnp.zeros_like(total)
        acc[j] = jnp.zeros((slot_rows, hd), jnp.float32)

        def step(b, carry):
            update(j, b, False)
            return carry

        lax.fori_loop(0, s, step, 0)
        update(j, s, True)
        acc[j] = acc[j] / total[...] * gates_ref[:, j : j + 1]

    for n in range(max(nz - 1, slots)):
        if n < slots:
            attend(n)
        if n < nz - 1:
            stage(WO, n + 1)

    for h in range(group_heads):
        value = jnp.zeros((slot_rows, hd), jnp.float32)
        for j in range(slots):
            value += jnp.where(heads_ref[:, j : j + 1] == h, acc[j], 0.0)
        weighted[:, h * hd : (h + 1) * hd] = value.astype(jnp.bfloat16)

    def back_copy(b, k):
        to = peer(k)
        return pltpu.make_async_remote_copy(
            contrib.at[b, to], back.at[b, g],
            back_send.at[b * (ng - 1) + k - 1], back_recv.at[b * (ng - 1) + k - 1], (s, to), MESH,
        )

    def back_arrival(b, k):
        frm = peer(ng - k)
        return pltpu.make_async_remote_copy(
            contrib.at[b, g], back.at[b, frm],
            back_send.at[b * (ng - 1) + k - 1], back_recv.at[b * (ng - 1) + k - 1], (s, frm), MESH,
        )

    def give_back(i, carry):
        b = block_at(i)

        consume_from(WO, i)

        product = jnp.dot(weighted[...], wo[b], preferred_element_type=jnp.float32)
        contrib[b] = product.astype(jnp.bfloat16).reshape(ng, cap, out_cols)
        for k in range(1, ng):
            back_copy(b, k).start()
        back[b, g] = contrib[b, g]
        return carry

    lax.fori_loop(0, nb, give_back, 0)

    def combine(i, carry):
        b = block_at(i)
        for k in range(1, ng):
            back_arrival(b, k).wait_recv()
        mixed = jnp.dot(
            sel_ref[...], back[b].reshape(slot_rows, out_cols), preferred_element_type=jnp.float32
        )
        out_ref[:, pl.ds(pl.multiple_of(b * out_cols, 128), out_cols)] = mixed.astype(jnp.bfloat16)
        for k in range(1, ng):
            back_copy(b, k).wait_send()
        return carry

    lax.fori_loop(0, nb, combine, 0)

    for k in range(1, ng):
        kv_copy(k).wait_send()
        row_copy(k).wait_send()
    for t in (KV, WQ, WO):
        for zz in range(nz):
            @pl.when((zz <= z) & (z < nz - 1))
            def _():
                gather(t, zz, 0, (s + nx, g)).wait_send()

            @pl.when((zz >= z) & (z > 0))
            def _():
                gather(t, zz, 1, (s - nx, g)).wait_send()

            if zz in (0, nz - 1):
                for k in range(1, nx):
                    @pl.when(z == zz)
                    def _():
                        gather(t, zz, 1 + k, xs(k)).wait_send()

                    @pl.when(z != zz)
                    def _():
                        gather(t, zz, 1 + k, xs(k), 0).wait_send()
            else:
                for k in range(1, nx):
                    gather(t, zz, 1 + k, xs(k)).wait_send()

        for k in range(1, nx):
            @pl.when(z < nz - 1)
            def _():
                half(t, 0, k).wait_send()

            @pl.when(z > 0)
            def _():
                half(t, 1, k).wait_send()


def on_device(nz, tokens, head_index, gate_fixed, kv_weight, query_weight, out_weight):
    groups = lax.axis_size("grp")
    nb = lax.axis_size("seq")
    nx = nb // nz
    tok_rows, model_width = tokens.shape
    capacity = 3 * tok_rows // groups
    head_width = kv_weight.shape[2] // 2
    group_heads = query_weight.shape[1] // head_width
    slots = head_index.shape[1] - 1
    offset = (lax.axis_index("seq") * groups + lax.axis_index("grp")) * tok_rows
    positions = offset + jnp.arange(tok_rows, dtype=jnp.int32)
    kv_local = jnp.einsum(
        "td,dgc->gtc", tokens, kv_weight, preferred_element_type=jnp.float32
    ).astype(jnp.bfloat16)
    selected, slot_head, slot_gate = route_tables(
        head_index, gate_fixed, groups, capacity, group_heads
    )
    by_slot = jnp.transpose(selected, (1, 2, 0))
    by_slot_bf = by_slot.astype(jnp.bfloat16)
    send_tokens = jnp.einsum(
        "gct,td->gcd", by_slot_bf, tokens, preferred_element_type=jnp.float32
    ).astype(jnp.bfloat16)
    send_pos = jnp.sum(by_slot * positions[None, None, :], axis=2)
    send_head = jnp.sum(
        by_slot[:, :, :, None] * jnp.transpose(slot_head, (1, 0, 2))[:, None, :, :], axis=2
    )
    send_gate = jnp.sum(
        by_slot[:, :, :, None] * jnp.transpose(slot_gate, (1, 0, 2))[:, None, :, :], axis=2
    )
    send_meta = jnp.concatenate([send_head, send_gate, send_pos[:, :, None]], axis=2)
    recv_meta = lax.all_to_all(send_meta, "grp", split_axis=0, concat_axis=0, tiled=True)
    slot_rows = groups * capacity
    recv_meta = recv_meta.reshape(slot_rows, 2 * slots + 1)
    heads = recv_meta[:, :slots]
    gates = recv_meta[:, slots : 2 * slots].astype(jnp.float32) / 32768.0
    slot_pos = recv_meta[:, 2 * slots :]
    sel = by_slot_bf.reshape(slot_rows, tok_rows).T
    bf, f32 = jnp.bfloat16, jnp.float32
    depth, q_cols = query_weight.shape
    out_cols = out_weight.shape[1]
    any_spec = pl.BlockSpec(memory_space=pl.ANY)
    vmem_spec = pl.BlockSpec(memory_space=pltpu.VMEM)
    dma = pltpu.SemaphoreType.DMA
    return pl.pallas_call(
        functools.partial(kernel, nz, nx, groups, group_heads, slots),
        out_shape=jax.ShapeDtypeStruct((tok_rows, model_width), bf),
        in_specs=[any_spec] * 4 + [vmem_spec] * 4,
        out_specs=vmem_spec,
        scratch_shapes=[
            pltpu.VMEM((groups, capacity, model_width), bf),
            pltpu.VMEM((nb, groups, tok_rows, 2 * head_width), bf),
            pltpu.VMEM((nb, depth, q_cols), bf),
            pltpu.VMEM((nb, q_cols, out_cols), bf),
            pltpu.VMEM((slot_rows, q_cols), f32),
            pltpu.VMEM((slots, slot_rows, head_width), bf),
            pltpu.VMEM((slots, slot_rows, head_width), f32),
            pltpu.VMEM((slot_rows, 1), f32),
            pltpu.VMEM((slot_rows, 1), f32),
            pltpu.VMEM((slot_rows, q_cols), bf),
            pltpu.VMEM((nb, groups, capacity, out_cols), bf),
            pltpu.VMEM((nb, groups, capacity, out_cols), bf),
            dma((4,)),
            dma((groups - 1,)),
            dma((groups - 1,)),
            dma((groups - 1,)),
            dma((groups - 1,)),
            dma((3 * nz * (nx + 1),)),
            dma((3 * nb,)),
            dma((nb * (groups - 1),)),
            dma((nb * (groups - 1),)),
            dma((3 * 2 * nx,)),
            dma((3 * 2 * nx,)),
        ],
        compiler_params=pltpu.CompilerParams(
            collective_id=0, has_side_effects=True, vmem_limit_bytes=56 * 2**20
        ),
    )(send_tokens, kv_local, query_weight, out_weight, heads, gates, slot_pos, sel)


def solution(mesh):
    in_specs = (
        P(("seq", "grp"), None),
        P(("seq", "grp"), None),
        P(("seq", "grp"), None),
        P(),
        P("seq", "grp"),
        P("grp", "seq"),
    )
    out_specs = P(("seq", "grp"), None)
    nz = 4 if mesh.shape["seq"] % 4 == 0 else mesh.shape["seq"]
    return jax.shard_map(
        functools.partial(on_device, nz),
        mesh=mesh, in_specs=in_specs, out_specs=out_specs, check_vma=False,
    )
```

```python
import functools

import jax
import jax.numpy as jnp
from jax import lax
from jax.experimental import pallas as pl
from jax.experimental.pallas import tpu as pltpu
from jax.sharding import PartitionSpec as P


def route_tables(head_index, gate_fixed, groups, capacity, group_heads):
    slots = head_index.shape[1] - 1
    cluster_membership = head_index // group_heads
    local_head = head_index % group_heads
    in_group = cluster_membership[:, None, :] == jnp.arange(groups, dtype=jnp.int32)[None, :, None]
    slot_order = jnp.cumsum(in_group.astype(jnp.int32), axis=2) - 1
    picked = (
        in_group[:, :, :, None] & (slot_order[:, :, :, None] == jnp.arange(slots, dtype=jnp.int32))
    ).astype(jnp.int32)
    slot_head = jnp.sum(picked * local_head[:, None, :, None], axis=2)
    slot_gate = jnp.sum(picked * gate_fixed[:, None, :, None], axis=2)
    member = jnp.any(in_group, axis=2).astype(jnp.int32)
    ranking = jnp.cumsum(member, axis=0) - 1
    retained = (member > 0) & (ranking < capacity)
    selected = (
        retained[:, :, None] & (ranking[:, :, None] == jnp.arange(capacity, dtype=jnp.int32))
    ).astype(jnp.int32)
    return (selected, slot_head, slot_gate)


MESH = pl.DeviceIdType.MESH
KV, WQ, WO = 0, 1, 2


def kernel(
    nz, nx, ng, group_heads, slots,
    kv_in, wq_in, wo_in, tokens_ref, sel_ref, meta_in,
    out_ref,
    rows, kvs, wq, wo, q_all, queries, acc, top, total, weighted, contrib, back,
    local_sem, row_send, row_recv, kv_send, kv_recv, gather_send, gather_recv, back_send, back_recv,
    half_send, half_recv, rows_in, meta, meta_send, meta_recv, sel_t,
):
    nb = nz * nx
    s, g = lax.axis_index("seq"), lax.axis_index("grp")
    z, x = s // nx, s % nx
    _, cap, width = rows.shape
    slot_rows = ng * cap
    depth = wq.shape[1]
    out_cols = wo.shape[2]
    tok = kvs.shape[2]
    keys = ng * tok
    hd = kvs.shape[3] // 2
    bufs = (kvs, wq, wo)

    def xs(k):
        return (z * nx + (x + k) % nx, g)

    def peer(k):
        return (g + k) % ng

    barrier = pltpu.get_barrier_semaphore()

    def greet(dev):
        pl.semaphore_signal(barrier, inc=1, device_id=dev, device_id_type=MESH)

    for k in range(1, nx):
        greet(xs(k))
    for k in range(1, ng):
        greet((s, peer(k)))

    @pl.when(z > 0)
    def _():
        greet((s - nx, g))

    @pl.when(z < nz - 1)
    def _():
        greet((s + nx, g))

    peers = nx - 1 + ng - 1 + (z > 0).astype(jnp.int32) + (z < nz - 1).astype(jnp.int32)
    pl.semaphore_wait(barrier, peers)

    own = [
        pltpu.make_async_copy(wq_in, wq.at[s], local_sem.at[0]),
        pltpu.make_async_copy(kv_in.at[g], kvs.at[s, g], local_sem.at[1]),
        pltpu.make_async_copy(wo_in, wo.at[s], local_sem.at[2]),
    ]
    for copy in own:
        copy.start()

    def kv_copy(k):
        to = peer(k)
        return pltpu.make_async_remote_copy(
            kv_in.at[to], kvs.at[s, g], kv_send.at[k - 1], kv_recv.at[k - 1], (s, to), MESH
        )

    def kv_arrival(k):
        frm = peer(ng - k)
        return pltpu.make_async_remote_copy(
            kv_in.at[g], kvs.at[s, frm], kv_send.at[k - 1], kv_recv.at[k - 1], (s, frm), MESH
        )

    def meta_copy(k):
        to = peer(k)
        return pltpu.make_async_remote_copy(
            meta_in.at[to], meta.at[g], meta_send.at[k - 1], meta_recv.at[k - 1], (s, to), MESH
        )

    def meta_arrival(k):
        frm = peer(ng - k)
        return pltpu.make_async_remote_copy(
            meta_in.at[g], meta.at[frm], meta_send.at[k - 1], meta_recv.at[k - 1], (s, frm), MESH
        )

    def row_copy(k):
        to = peer(k)
        return pltpu.make_async_remote_copy(
            rows_in.at[to], rows.at[g], row_send.at[k - 1], row_recv.at[k - 1], (s, to), MESH
        )

    def row_arrival(k):
        frm = peer(ng - k)
        return pltpu.make_async_remote_copy(
            rows_in.at[g], rows.at[frm], row_send.at[k - 1], row_recv.at[k - 1], (s, frm), MESH
        )

    def part(t, b, which):
        if which is None:
            return bufs[t].at[b]
        rows_half = bufs[t].shape[1] // 2
        return bufs[t].at[b, which * rows_half : (which + 1) * rows_half]

    def is_end(zz):
        return (zz == 0) | (zz == nz - 1)

    def gather(t, zz, kind, dev, which=None):
        here = part(t, zz * nx + x, which)
        return pltpu.make_async_remote_copy(
            here, here,
            gather_send.at[(t * nz + zz) * (nx + 1) + kind],
            gather_recv.at[t * nb + zz * nx + x], dev, MESH,
        )

    def arrival(t, b, which=None):
        here = part(t, b, which)
        return pltpu.make_async_remote_copy(
            here, here, gather_send.at[0], gather_recv.at[t * nb + b], (s, peer(1)), MESH
        )

    def half(t, way, k):
        end = 0 if way == 0 else nz - 1
        here = part(t, end * nx + (x + k) % nx, 1)
        at = (t * 2 + way) * nx + k
        to = s + nx if way == 0 else s - nx
        return pltpu.make_async_remote_copy(
            here, here, half_send.at[at], half_recv.at[at], (to, g), MESH
        )

    def half_arrival(t, way, k):
        end = 0 if way == 0 else nz - 1
        here = part(t, end * nx + (x + k) % nx, 1)
        at = (t * 2 + way) * nx + k
        return pltpu.make_async_remote_copy(
            here, here, half_send.at[at], half_recv.at[at], (s, peer(1)), MESH
        )

    def up(t, zz):
        @pl.when(z < nz - 1)
        def _():
            gather(t, zz, 0, (s + nx, g)).start()

    def down(t, zz):
        @pl.when(z > 0)
        def _():
            gather(t, zz, 1, (s - nx, g)).start()

    def send_own(t):
        up(t, z)
        down(t, z)
        for k in range(1, nx):
            gather(t, z, 1 + k, xs(k)).start()

    def across(t, zz):
        @pl.when(is_end(zz))
        def _():
            for k in range(1, nx):
                gather(t, zz, 1 + k, xs(k), 0).start()

        @pl.when(jnp.logical_not(is_end(zz)))
        def _():
            for k in range(1, nx):
                gather(t, zz, 1 + k, xs(k)).start()

    def column_stage(t, d):
        @pl.when(z - d >= 0)
        def _():
            arrival(t, (z - d) * nx + x).wait_recv()
            up(t, z - d)
            across(t, z - d)

        @pl.when(z + d < nz)
        def _():
            arrival(t, (z + d) * nx + x).wait_recv()
            down(t, z + d)
            across(t, z + d)

    def half_stage(t, e):
        for way in (0, 1):
            @pl.when(z == (e if way == 0 else nz - 1 - e))
            def _():
                for k in range(1, nx):
                    if e == 0:
                        arrival(t, z * nx + (x + k) % nx).wait_recv()
                    else:
                        half_arrival(t, way, k).wait_recv()
                    half(t, way, k).start()

    def stage(t, d):
        column_stage(t, d)
        if d == 1:
            half_stage(t, 0)
        if d < nz - 1:
            half_stage(t, d)

    def consume(t, zz, k):
        b = zz * nx + (x + k) % nx

        @pl.when((zz == z) & jnp.logical_not(is_end(z)))
        def _():
            arrival(t, b).wait_recv()

        @pl.when((zz != z) & jnp.logical_not(is_end(zz)))
        def _():
            arrival(t, b).wait_recv()

        @pl.when((zz != z) & is_end(zz))
        def _():
            arrival(t, b, 0).wait_recv()

        @pl.when((zz == 0) & (z == nz - 1))
        def _():
            half_arrival(t, 0, k).wait_recv()

        @pl.when((zz == nz - 1) & (z == 0))
        def _():
            half_arrival(t, 1, k).wait_recv()

    for k in range(1, ng):
        kv_copy(k).start()
    own[0].wait()
    send_own(WQ)
    for k in range(1, ng):
        meta_copy(k).start()
    own[1].wait()
    for k in range(1, ng):
        kv_arrival(k).wait_recv()
    send_own(KV)

    def pick(i, carry):
        cols = pl.ds(pl.multiple_of(i * 512, 128), 512)
        piece = jnp.dot(sel_ref[...], tokens_ref[:, cols], preferred_element_type=jnp.float32)
        rows_in[:, :, cols] = piece.astype(jnp.bfloat16).reshape(ng, cap, 512)
        return carry

    lax.fori_loop(0, width // 512, pick, 0)
    for k in range(1, ng):
        row_copy(k).start()
    rows[g] = rows_in[g]
    meta[g] = meta_in[g]
    sel_t[...] = sel_ref[...].astype(jnp.float32).T.astype(jnp.bfloat16)
    own[2].wait()
    for d in range(1, nz):
        stage(KV, d)
        stage(WQ, d)
        if d == max(nz - 2, 1):
            send_own(WO)

    for k in range(1, ng):
        row_arrival(k).wait_recv()
        meta_arrival(k).wait_recv()

    def shard_at(i):
        return jnp.where(z * 2 < nz, i % nz, nz - 1 - i % nz)

    def block_at(i):
        return shard_at(i) * nx + (x + i // nz) % nx

    def consume_from(t, i):
        for k in range(1, nx):
            @pl.when(i // nz == k)
            def _():
                consume(t, shard_at(i), k)

    q_all[...] = jnp.zeros_like(q_all)

    def project(i, carry):
        b = block_at(i)

        consume_from(WQ, i)

        piece = rows[:, :, pl.ds(pl.multiple_of(b * depth, 128), depth)].reshape(slot_rows, depth)
        q_all[...] += jnp.dot(piece, wq[b], preferred_element_type=jnp.float32)
        return carry

    lax.fori_loop(0, nz, project, 0)
    column_stage(WO, 1)
    lax.fori_loop(nz, nb, project, 0)

    def meta_column(i):
        return meta[:, :, i : i + 1].reshape(slot_rows, 1)

    for j in range(slots):
        head = meta_column(j)
        q = jnp.zeros((slot_rows, hd), jnp.float32)
        for h in range(group_heads):
            q = jnp.where(head == h, q_all[:, h * hd : (h + 1) * hd], q)
        queries[j] = q.astype(jnp.bfloat16)

    for k in range(1, nx):
        for zz in range(nz):
            consume(KV, zz, k)

    def update(j, b, masked):
        k = kvs[b, :, :, :hd].reshape(keys, hd)
        v = kvs[b, :, :, hd:].reshape(keys, hd)
        scores = lax.dot_general(
            queries[j], k, (((1,), (1,)), ((), ())), preferred_element_type=jnp.float32
        ) * (hd ** -0.5)
        if masked:
            key_pos = b * keys + lax.broadcasted_iota(jnp.int32, scores.shape, 1)
            scores = jnp.where(key_pos <= meta_column(2 * slots), scores, -1e30)
        before = top[...]
        newest = jnp.maximum(before, jnp.max(scores, axis=1, keepdims=True))
        weights = jnp.exp(scores - newest)
        factor = jnp.exp(before - newest)
        total[...] = total[...] * factor + jnp.sum(weights, axis=1, keepdims=True)
        acc[j] = acc[j] * factor + jnp.dot(
            weights.astype(jnp.bfloat16), v, preferred_element_type=jnp.float32
        )
        top[...] = newest

    def attend(j):
        top[...] = jnp.full_like(top, -1e30)
        total[...] = jnp.zeros_like(total)
        acc[j] = jnp.zeros((slot_rows, hd), jnp.float32)

        def step(b, carry):
            update(j, b, False)
            return carry

        lax.fori_loop(0, s, step, 0)
        update(j, s, True)
        acc[j] = acc[j] / total[...] * (meta_column(slots + j).astype(jnp.float32) / 32768.0)

    for n in range(max(nz - 1, slots)):
        if n < slots:
            attend(n)
        if n == 0:
            half_stage(WO, 0)
            if nz > 2:
                half_stage(WO, 1)
        elif n < nz - 1:
            stage(WO, n + 1)

    for h in range(group_heads):
        value = jnp.zeros((slot_rows, hd), jnp.float32)
        for j in range(slots):
            value += jnp.where(meta_column(j) == h, acc[j], 0.0)
        weighted[:, h * hd : (h + 1) * hd] = value.astype(jnp.bfloat16)

    def back_copy(b, k):
        to = peer(k)
        return pltpu.make_async_remote_copy(
            contrib.at[b, to], back.at[b, g],
            back_send.at[b * (ng - 1) + k - 1], back_recv.at[b * (ng - 1) + k - 1], (s, to), MESH,
        )

    def back_arrival(b, k):
        frm = peer(ng - k)
        return pltpu.make_async_remote_copy(
            contrib.at[b, g], back.at[b, frm],
            back_send.at[b * (ng - 1) + k - 1], back_recv.at[b * (ng - 1) + k - 1], (s, frm), MESH,
        )

    def give_back(i, carry):
        b = block_at(i)

        consume_from(WO, i)

        product = jnp.dot(weighted[...], wo[b], preferred_element_type=jnp.float32)
        contrib[b] = product.astype(jnp.bfloat16).reshape(ng, cap, out_cols)
        for k in range(1, ng):
            back_copy(b, k).start()
        back[b, g] = contrib[b, g]
        return carry

    lax.fori_loop(0, nb, give_back, 0)

    def combine(i, carry):
        b = block_at(i)
        for k in range(1, ng):
            back_arrival(b, k).wait_recv()
        mixed = jnp.dot(
            sel_t[...], back[b].reshape(slot_rows, out_cols), preferred_element_type=jnp.float32
        )
        out_ref[:, pl.ds(pl.multiple_of(b * out_cols, 128), out_cols)] = mixed.astype(jnp.bfloat16)
        for k in range(1, ng):
            back_copy(b, k).wait_send()
        return carry

    lax.fori_loop(0, nb, combine, 0)

    for k in range(1, ng):
        kv_copy(k).wait_send()
        row_copy(k).wait_send()
        meta_copy(k).wait_send()
    for t in (KV, WQ, WO):
        for zz in range(nz):
            @pl.when((zz <= z) & (z < nz - 1))
            def _():
                gather(t, zz, 0, (s + nx, g)).wait_send()

            @pl.when((zz >= z) & (z > 0))
            def _():
                gather(t, zz, 1, (s - nx, g)).wait_send()

            if zz in (0, nz - 1):
                for k in range(1, nx):
                    @pl.when(z == zz)
                    def _():
                        gather(t, zz, 1 + k, xs(k)).wait_send()

                    @pl.when(z != zz)
                    def _():
                        gather(t, zz, 1 + k, xs(k), 0).wait_send()
            else:
                for k in range(1, nx):
                    gather(t, zz, 1 + k, xs(k)).wait_send()

        for k in range(1, nx):
            @pl.when(z < nz - 1)
            def _():
                half(t, 0, k).wait_send()

            @pl.when(z > 0)
            def _():
                half(t, 1, k).wait_send()


def on_device(nz, tokens, head_index, gate_fixed, kv_weight, query_weight, out_weight):
    groups = lax.axis_size("grp")
    nb = lax.axis_size("seq")
    nx = nb // nz
    tok_rows, model_width = tokens.shape
    capacity = 3 * tok_rows // groups
    head_width = kv_weight.shape[2] // 2
    group_heads = query_weight.shape[1] // head_width
    slots = head_index.shape[1] - 1
    offset = (lax.axis_index("seq") * groups + lax.axis_index("grp")) * tok_rows
    positions = offset + jnp.arange(tok_rows, dtype=jnp.int32)
    kv_local = jnp.einsum(
        "td,dgc->gtc", tokens, kv_weight, preferred_element_type=jnp.float32
    ).astype(jnp.bfloat16)
    selected, slot_head, slot_gate = route_tables(
        head_index, gate_fixed, groups, capacity, group_heads
    )
    by_slot = jnp.transpose(selected, (1, 2, 0))
    send_pos = jnp.sum(by_slot * positions[None, None, :], axis=2)
    send_head = jnp.sum(
        by_slot[:, :, :, None] * jnp.transpose(slot_head, (1, 0, 2))[:, None, :, :], axis=2
    )
    send_gate = jnp.sum(
        by_slot[:, :, :, None] * jnp.transpose(slot_gate, (1, 0, 2))[:, None, :, :], axis=2
    )
    send_meta = jnp.concatenate([send_head, send_gate, send_pos[:, :, None]], axis=2)
    send_meta = jnp.pad(send_meta, ((0, 0), (0, 0), (0, 128 - send_meta.shape[2])))
    slot_rows = groups * capacity
    sel = by_slot.astype(jnp.bfloat16).reshape(slot_rows, tok_rows)
    bf, f32 = jnp.bfloat16, jnp.float32
    depth, q_cols = query_weight.shape
    out_cols = out_weight.shape[1]
    any_spec = pl.BlockSpec(memory_space=pl.ANY)
    vmem_spec = pl.BlockSpec(memory_space=pltpu.VMEM)
    dma = pltpu.SemaphoreType.DMA
    return pl.pallas_call(
        functools.partial(kernel, nz, nx, groups, group_heads, slots),
        out_shape=jax.ShapeDtypeStruct((tok_rows, model_width), bf),
        in_specs=[any_spec] * 3 + [vmem_spec] * 3,
        out_specs=vmem_spec,
        scratch_shapes=[
            pltpu.VMEM((groups, capacity, model_width), bf),
            pltpu.VMEM((nb, groups, tok_rows, 2 * head_width), bf),
            pltpu.VMEM((nb, depth, q_cols), bf),
            pltpu.VMEM((nb, q_cols, out_cols), bf),
            pltpu.VMEM((slot_rows, q_cols), f32),
            pltpu.VMEM((slots, slot_rows, head_width), bf),
            pltpu.VMEM((slots, slot_rows, head_width), f32),
            pltpu.VMEM((slot_rows, 1), f32),
            pltpu.VMEM((slot_rows, 1), f32),
            pltpu.VMEM((slot_rows, q_cols), bf),
            pltpu.VMEM((nb, groups, capacity, out_cols), bf),
            pltpu.VMEM((nb, groups, capacity, out_cols), bf),
            dma((3,)),
            dma((groups - 1,)),
            dma((groups - 1,)),
            dma((groups - 1,)),
            dma((groups - 1,)),
            dma((3 * nz * (nx + 1),)),
            dma((3 * nb,)),
            dma((nb * (groups - 1),)),
            dma((nb * (groups - 1),)),
            dma((3 * 2 * nx,)),
            dma((3 * 2 * nx,)),
            pltpu.VMEM((groups, capacity, model_width), bf),
            pltpu.VMEM((groups, capacity, 128), jnp.int32),
            dma((groups - 1,)),
            dma((groups - 1,)),
            pltpu.VMEM((tok_rows, slot_rows), bf),
        ],
        compiler_params=pltpu.CompilerParams(
            collective_id=0, has_side_effects=True, vmem_limit_bytes=56 * 2**20
        ),
    )(kv_local, query_weight, out_weight, tokens, sel, send_meta)


def solution(mesh):
    in_specs = (
        P(("seq", "grp"), None),
        P(("seq", "grp"), None),
        P(("seq", "grp"), None),
        P(),
        P("seq", "grp"),
        P("grp", "seq"),
    )
    out_specs = P(("seq", "grp"), None)
    nz = 4 if mesh.shape["seq"] % 4 == 0 else mesh.shape["seq"]
    return jax.shard_map(
        functools.partial(on_device, nz),
        mesh=mesh, in_specs=in_specs, out_specs=out_specs, check_vma=False,
    )
```

```python
import functools

import jax
import jax.numpy as jnp
from jax import lax
from jax.experimental import pallas as pl
from jax.experimental.pallas import tpu as pltpu
from jax.sharding import PartitionSpec as P


def route_tables(head_index, gate_fixed, groups, capacity, group_heads):
    slots = head_index.shape[1] - 1
    cluster_membership = head_index // group_heads
    local_head = head_index % group_heads
    in_group = cluster_membership[:, None, :] == jnp.arange(groups, dtype=jnp.int32)[None, :, None]
    slot_order = jnp.cumsum(in_group.astype(jnp.int32), axis=2) - 1
    picked = (
        in_group[:, :, :, None] & (slot_order[:, :, :, None] == jnp.arange(slots, dtype=jnp.int32))
    ).astype(jnp.int32)
    slot_head = jnp.sum(picked * local_head[:, None, :, None], axis=2)
    slot_gate = jnp.sum(picked * gate_fixed[:, None, :, None], axis=2)
    member = jnp.any(in_group, axis=2).astype(jnp.int32)
    ranking = jnp.cumsum(member, axis=0) - 1
    retained = (member > 0) & (ranking < capacity)
    selected = (
        retained[:, :, None] & (ranking[:, :, None] == jnp.arange(capacity, dtype=jnp.int32))
    ).astype(jnp.int32)
    return (selected, slot_head, slot_gate)


MESH = pl.DeviceIdType.MESH
KV, WQ, WO = 0, 1, 2


def kernel(
    nz, nx, ng, group_heads, slots,
    kv_in, wq_in, wo_in, tokens_ref, sel_ref, meta_in,
    out_ref,
    rows, kvs, wq, wo, q_all, queries, acc, top, total, weighted, contrib, back,
    local_sem, row_send, row_recv, kv_send, kv_recv, gather_send, gather_recv, back_send, back_recv,
    half_send, half_recv, rows_in, meta, meta_send, meta_recv, sel_t,
):
    nb = nz * nx
    s, g = lax.axis_index("seq"), lax.axis_index("grp")
    z, x = s // nx, s % nx
    _, cap, width = rows.shape
    slot_rows = ng * cap
    depth = wq.shape[1]
    out_cols = wo.shape[2]
    tok = kvs.shape[2]
    keys = ng * tok
    hd = kvs.shape[3] // 2
    bufs = (kvs, wq, wo)

    def xs(k):
        return (z * nx + (x + k) % nx, g)

    def peer(k):
        return (g + k) % ng

    barrier = pltpu.get_barrier_semaphore()

    def greet(dev):
        pl.semaphore_signal(barrier, inc=1, device_id=dev, device_id_type=MESH)

    for k in range(1, nx):
        greet(xs(k))
    for k in range(1, ng):
        greet((s, peer(k)))

    @pl.when(z > 0)
    def _():
        greet((s - nx, g))

    @pl.when(z < nz - 1)
    def _():
        greet((s + nx, g))

    peers = nx - 1 + ng - 1 + (z > 0).astype(jnp.int32) + (z < nz - 1).astype(jnp.int32)
    pl.semaphore_wait(barrier, peers)

    own = [
        pltpu.make_async_copy(wq_in, wq.at[s], local_sem.at[0]),
        pltpu.make_async_copy(kv_in.at[g], kvs.at[s, g], local_sem.at[1]),
        pltpu.make_async_copy(wo_in, wo.at[s], local_sem.at[2]),
    ]
    for copy in own:
        copy.start()

    def kv_copy(k):
        to = peer(k)
        return pltpu.make_async_remote_copy(
            kv_in.at[to], kvs.at[s, g], kv_send.at[k - 1], kv_recv.at[k - 1], (s, to), MESH
        )

    def kv_arrival(k):
        frm = peer(ng - k)
        return pltpu.make_async_remote_copy(
            kv_in.at[g], kvs.at[s, frm], kv_send.at[k - 1], kv_recv.at[k - 1], (s, frm), MESH
        )

    def meta_copy(k):
        to = peer(k)
        return pltpu.make_async_remote_copy(
            meta_in.at[to], meta.at[g], meta_send.at[k - 1], meta_recv.at[k - 1], (s, to), MESH
        )

    def meta_arrival(k):
        frm = peer(ng - k)
        return pltpu.make_async_remote_copy(
            meta_in.at[g], meta.at[frm], meta_send.at[k - 1], meta_recv.at[k - 1], (s, frm), MESH
        )

    def row_copy(k):
        to = peer(k)
        return pltpu.make_async_remote_copy(
            rows_in.at[to], rows.at[g], row_send.at[k - 1], row_recv.at[k - 1], (s, to), MESH
        )

    def row_arrival(k):
        frm = peer(ng - k)
        return pltpu.make_async_remote_copy(
            rows_in.at[g], rows.at[frm], row_send.at[k - 1], row_recv.at[k - 1], (s, frm), MESH
        )

    def part(t, b, which):
        if which is None:
            return bufs[t].at[b]
        rows_half = bufs[t].shape[1] // 2
        return bufs[t].at[b, which * rows_half : (which + 1) * rows_half]

    def is_end(zz):
        return (zz == 0) | (zz == nz - 1)

    def gather(t, zz, kind, dev, which=None):
        here = part(t, zz * nx + x, which)
        return pltpu.make_async_remote_copy(
            here, here,
            gather_send.at[(t * nz + zz) * (nx + 1) + kind],
            gather_recv.at[t * nb + zz * nx + x], dev, MESH,
        )

    def arrival(t, b, which=None):
        here = part(t, b, which)
        return pltpu.make_async_remote_copy(
            here, here, gather_send.at[0], gather_recv.at[t * nb + b], (s, peer(1)), MESH
        )

    def half(t, way, k):
        end = 0 if way == 0 else nz - 1
        here = part(t, end * nx + (x + k) % nx, 1)
        at = (t * 2 + way) * nx + k
        to = s + nx if way == 0 else s - nx
        return pltpu.make_async_remote_copy(
            here, here, half_send.at[at], half_recv.at[at], (to, g), MESH
        )

    def half_arrival(t, way, k):
        end = 0 if way == 0 else nz - 1
        here = part(t, end * nx + (x + k) % nx, 1)
        at = (t * 2 + way) * nx + k
        return pltpu.make_async_remote_copy(
            here, here, half_send.at[at], half_recv.at[at], (s, peer(1)), MESH
        )

    def up(t, zz):
        @pl.when(z < nz - 1)
        def _():
            gather(t, zz, 0, (s + nx, g)).start()

    def down(t, zz):
        @pl.when(z > 0)
        def _():
            gather(t, zz, 1, (s - nx, g)).start()

    def send_own(t):
        up(t, z)
        down(t, z)
        for k in range(1, nx):
            gather(t, z, 1 + k, xs(k)).start()

    def across(t, zz):
        @pl.when(is_end(zz))
        def _():
            for k in range(1, nx):
                gather(t, zz, 1 + k, xs(k), 0).start()

        @pl.when(jnp.logical_not(is_end(zz)))
        def _():
            for k in range(1, nx):
                gather(t, zz, 1 + k, xs(k)).start()

    def column_stage(t, d):
        @pl.when(z - d >= 0)
        def _():
            arrival(t, (z - d) * nx + x).wait_recv()
            up(t, z - d)
            across(t, z - d)

        @pl.when(z + d < nz)
        def _():
            arrival(t, (z + d) * nx + x).wait_recv()
            down(t, z + d)
            across(t, z + d)

    def half_stage(t, e):
        for way in (0, 1):
            @pl.when(z == (e if way == 0 else nz - 1 - e))
            def _():
                for k in range(1, nx):
                    if e == 0:
                        arrival(t, z * nx + (x + k) % nx).wait_recv()
                    else:
                        half_arrival(t, way, k).wait_recv()
                    half(t, way, k).start()

    def stage(t, d):
        column_stage(t, d)
        if d == 1:
            half_stage(t, 0)
        if d < nz - 1:
            half_stage(t, d)

    def consume(t, zz, k):
        b = zz * nx + (x + k) % nx

        @pl.when((zz == z) & jnp.logical_not(is_end(z)))
        def _():
            arrival(t, b).wait_recv()

        @pl.when((zz != z) & jnp.logical_not(is_end(zz)))
        def _():
            arrival(t, b).wait_recv()

        @pl.when((zz != z) & is_end(zz))
        def _():
            arrival(t, b, 0).wait_recv()

        @pl.when((zz == 0) & (z == nz - 1))
        def _():
            half_arrival(t, 0, k).wait_recv()

        @pl.when((zz == nz - 1) & (z == 0))
        def _():
            half_arrival(t, 1, k).wait_recv()

    for k in range(1, ng):
        kv_copy(k).start()
    own[0].wait()
    send_own(WQ)
    for k in range(1, ng):
        meta_copy(k).start()
    own[1].wait()
    for k in range(1, ng):
        kv_arrival(k).wait_recv()
    send_own(KV)

    def pick(i, carry):
        cols = pl.ds(pl.multiple_of(i * 512, 128), 512)
        piece = jnp.dot(sel_ref[...], tokens_ref[:, cols], preferred_element_type=jnp.float32)
        rows_in[:, :, cols] = piece.astype(jnp.bfloat16).reshape(ng, cap, 512)
        return carry

    lax.fori_loop(0, width // 512, pick, 0)
    for k in range(1, ng):
        row_copy(k).start()
    rows[g] = rows_in[g]
    meta[g] = meta_in[g]
    sel_t[...] = sel_ref[...].astype(jnp.float32).T.astype(jnp.bfloat16)
    own[2].wait()
    for d in range(1, nz):
        stage(KV, d)
        stage(WQ, d)
        if d == 1:
            send_own(WO)
        if d == max(nz - 2, 1):
            column_stage(WO, 1)
    half_stage(WO, 0)
    if nz > 2:
        half_stage(WO, 1)

    for k in range(1, ng):
        row_arrival(k).wait_recv()
        meta_arrival(k).wait_recv()

    def shard_at(i):
        return jnp.where(z * 2 < nz, i % nz, nz - 1 - i % nz)

    def block_at(i):
        return shard_at(i) * nx + (x + i // nz) % nx

    def consume_from(t, i):
        for k in range(1, nx):
            @pl.when(i // nz == k)
            def _():
                consume(t, shard_at(i), k)

    q_all[...] = jnp.zeros_like(q_all)

    def project(i, carry):
        b = block_at(i)

        consume_from(WQ, i)

        piece = rows[:, :, pl.ds(pl.multiple_of(b * depth, 128), depth)].reshape(slot_rows, depth)
        q_all[...] += jnp.dot(piece, wq[b], preferred_element_type=jnp.float32)
        return carry

    lax.fori_loop(0, nb, project, 0)

    def meta_column(i):
        return meta[:, :, i : i + 1].reshape(slot_rows, 1)

    for j in range(slots):
        head = meta_column(j)
        q = jnp.zeros((slot_rows, hd), jnp.float32)
        for h in range(group_heads):
            q = jnp.where(head == h, q_all[:, h * hd : (h + 1) * hd], q)
        queries[j] = q.astype(jnp.bfloat16)

    for k in range(1, nx):
        for zz in range(nz):
            consume(KV, zz, k)

    def update(j, b, masked):
        k = kvs[b, :, :, :hd].reshape(keys, hd)
        v = kvs[b, :, :, hd:].reshape(keys, hd)
        scores = lax.dot_general(
            queries[j], k, (((1,), (1,)), ((), ())), preferred_element_type=jnp.float32
        ) * (hd ** -0.5)
        if masked:
            key_pos = b * keys + lax.broadcasted_iota(jnp.int32, scores.shape, 1)
            scores = jnp.where(key_pos <= meta_column(2 * slots), scores, -1e30)
        before = top[...]
        newest = jnp.maximum(before, jnp.max(scores, axis=1, keepdims=True))
        weights = jnp.exp(scores - newest)
        factor = jnp.exp(before - newest)
        total[...] = total[...] * factor + jnp.sum(weights, axis=1, keepdims=True)
        acc[j] = acc[j] * factor + jnp.dot(
            weights.astype(jnp.bfloat16), v, preferred_element_type=jnp.float32
        )
        top[...] = newest

    def attend(j):
        top[...] = jnp.full_like(top, -1e30)
        total[...] = jnp.zeros_like(total)
        acc[j] = jnp.zeros((slot_rows, hd), jnp.float32)

        def step(b, carry):
            update(j, b, False)
            return carry

        lax.fori_loop(0, s, step, 0)
        update(j, s, True)
        acc[j] = acc[j] / total[...] * (meta_column(slots + j).astype(jnp.float32) / 32768.0)

    for n in range(max(nz - 1, slots)):
        if n < slots:
            attend(n)
        if 0 < n < nz - 1:
            stage(WO, n + 1)

    for h in range(group_heads):
        value = jnp.zeros((slot_rows, hd), jnp.float32)
        for j in range(slots):
            value += jnp.where(meta_column(j) == h, acc[j], 0.0)
        weighted[:, h * hd : (h + 1) * hd] = value.astype(jnp.bfloat16)

    def back_copy(b, k):
        to = peer(k)
        return pltpu.make_async_remote_copy(
            contrib.at[b, to], back.at[b, g],
            back_send.at[b * (ng - 1) + k - 1], back_recv.at[b * (ng - 1) + k - 1], (s, to), MESH,
        )

    def back_arrival(b, k):
        frm = peer(ng - k)
        return pltpu.make_async_remote_copy(
            contrib.at[b, g], back.at[b, frm],
            back_send.at[b * (ng - 1) + k - 1], back_recv.at[b * (ng - 1) + k - 1], (s, frm), MESH,
        )

    def give_back(i, carry):
        b = block_at(i)

        consume_from(WO, i)

        product = jnp.dot(weighted[...], wo[b], preferred_element_type=jnp.float32)
        contrib[b] = product.astype(jnp.bfloat16).reshape(ng, cap, out_cols)
        for k in range(1, ng):
            back_copy(b, k).start()
        back[b, g] = contrib[b, g]
        return carry

    lax.fori_loop(0, nb, give_back, 0)

    def combine(i, carry):
        b = block_at(i)
        for k in range(1, ng):
            back_arrival(b, k).wait_recv()
        mixed = jnp.dot(
            sel_t[...], back[b].reshape(slot_rows, out_cols), preferred_element_type=jnp.float32
        )
        out_ref[:, pl.ds(pl.multiple_of(b * out_cols, 128), out_cols)] = mixed.astype(jnp.bfloat16)
        for k in range(1, ng):
            back_copy(b, k).wait_send()
        return carry

    lax.fori_loop(0, nb, combine, 0)

    for k in range(1, ng):
        kv_copy(k).wait_send()
        row_copy(k).wait_send()
        meta_copy(k).wait_send()
    for t in (KV, WQ, WO):
        for zz in range(nz):
            @pl.when((zz <= z) & (z < nz - 1))
            def _():
                gather(t, zz, 0, (s + nx, g)).wait_send()

            @pl.when((zz >= z) & (z > 0))
            def _():
                gather(t, zz, 1, (s - nx, g)).wait_send()

            if zz in (0, nz - 1):
                for k in range(1, nx):
                    @pl.when(z == zz)
                    def _():
                        gather(t, zz, 1 + k, xs(k)).wait_send()

                    @pl.when(z != zz)
                    def _():
                        gather(t, zz, 1 + k, xs(k), 0).wait_send()
            else:
                for k in range(1, nx):
                    gather(t, zz, 1 + k, xs(k)).wait_send()

        for k in range(1, nx):
            @pl.when(z < nz - 1)
            def _():
                half(t, 0, k).wait_send()

            @pl.when(z > 0)
            def _():
                half(t, 1, k).wait_send()


def on_device(nz, tokens, head_index, gate_fixed, kv_weight, query_weight, out_weight):
    groups = lax.axis_size("grp")
    nb = lax.axis_size("seq")
    nx = nb // nz
    tok_rows, model_width = tokens.shape
    capacity = 3 * tok_rows // groups
    head_width = kv_weight.shape[2] // 2
    group_heads = query_weight.shape[1] // head_width
    slots = head_index.shape[1] - 1
    offset = (lax.axis_index("seq") * groups + lax.axis_index("grp")) * tok_rows
    positions = offset + jnp.arange(tok_rows, dtype=jnp.int32)
    kv_local = jnp.einsum(
        "td,dgc->gtc", tokens, kv_weight, preferred_element_type=jnp.float32
    ).astype(jnp.bfloat16)
    selected, slot_head, slot_gate = route_tables(
        head_index, gate_fixed, groups, capacity, group_heads
    )
    by_slot = jnp.transpose(selected, (1, 2, 0))
    send_pos = jnp.sum(by_slot * positions[None, None, :], axis=2)
    send_head = jnp.sum(
        by_slot[:, :, :, None] * jnp.transpose(slot_head, (1, 0, 2))[:, None, :, :], axis=2
    )
    send_gate = jnp.sum(
        by_slot[:, :, :, None] * jnp.transpose(slot_gate, (1, 0, 2))[:, None, :, :], axis=2
    )
    send_meta = jnp.concatenate([send_head, send_gate, send_pos[:, :, None]], axis=2)
    send_meta = jnp.pad(send_meta, ((0, 0), (0, 0), (0, 128 - send_meta.shape[2])))
    slot_rows = groups * capacity
    sel = by_slot.astype(jnp.bfloat16).reshape(slot_rows, tok_rows)
    bf, f32 = jnp.bfloat16, jnp.float32
    depth, q_cols = query_weight.shape
    out_cols = out_weight.shape[1]
    any_spec = pl.BlockSpec(memory_space=pl.ANY)
    vmem_spec = pl.BlockSpec(memory_space=pltpu.VMEM)
    dma = pltpu.SemaphoreType.DMA
    return pl.pallas_call(
        functools.partial(kernel, nz, nx, groups, group_heads, slots),
        out_shape=jax.ShapeDtypeStruct((tok_rows, model_width), bf),
        in_specs=[any_spec] * 3 + [vmem_spec] * 3,
        out_specs=vmem_spec,
        scratch_shapes=[
            pltpu.VMEM((groups, capacity, model_width), bf),
            pltpu.VMEM((nb, groups, tok_rows, 2 * head_width), bf),
            pltpu.VMEM((nb, depth, q_cols), bf),
            pltpu.VMEM((nb, q_cols, out_cols), bf),
            pltpu.VMEM((slot_rows, q_cols), f32),
            pltpu.VMEM((slots, slot_rows, head_width), bf),
            pltpu.VMEM((slots, slot_rows, head_width), f32),
            pltpu.VMEM((slot_rows, 1), f32),
            pltpu.VMEM((slot_rows, 1), f32),
            pltpu.VMEM((slot_rows, q_cols), bf),
            pltpu.VMEM((nb, groups, capacity, out_cols), bf),
            pltpu.VMEM((nb, groups, capacity, out_cols), bf),
            dma((3,)),
            dma((groups - 1,)),
            dma((groups - 1,)),
            dma((groups - 1,)),
            dma((groups - 1,)),
            dma((3 * nz * (nx + 1),)),
            dma((3 * nb,)),
            dma((nb * (groups - 1),)),
            dma((nb * (groups - 1),)),
            dma((3 * 2 * nx,)),
            dma((3 * 2 * nx,)),
            pltpu.VMEM((groups, capacity, model_width), bf),
            pltpu.VMEM((groups, capacity, 128), jnp.int32),
            dma((groups - 1,)),
            dma((groups - 1,)),
            pltpu.VMEM((tok_rows, slot_rows), bf),
        ],
        compiler_params=pltpu.CompilerParams(
            collective_id=0, has_side_effects=True, vmem_limit_bytes=56 * 2**20
        ),
    )(kv_local, query_weight, out_weight, tokens, sel, send_meta)


def solution(mesh):
    in_specs = (
        P(("seq", "grp"), None),
        P(("seq", "grp"), None),
        P(("seq", "grp"), None),
        P(),
        P("seq", "grp"),
        P("grp", "seq"),
    )
    out_specs = P(("seq", "grp"), None)
    nz = 4 if mesh.shape["seq"] % 4 == 0 else mesh.shape["seq"]
    return jax.shard_map(
        functools.partial(on_device, nz),
        mesh=mesh, in_specs=in_specs, out_specs=out_specs, check_vma=False,
    )
```

```python
import functools

import jax
import jax.numpy as jnp
from jax import lax
from jax.experimental import pallas as pl
from jax.experimental.pallas import tpu as pltpu
from jax.sharding import PartitionSpec as P


def route_tables(head_index, gate_fixed, groups, capacity, group_heads):
    slots = head_index.shape[1] - 1
    cluster_membership = head_index // group_heads
    local_head = head_index % group_heads
    in_group = cluster_membership[:, None, :] == jnp.arange(groups, dtype=jnp.int32)[None, :, None]
    slot_order = jnp.cumsum(in_group.astype(jnp.int32), axis=2) - 1
    picked = (
        in_group[:, :, :, None] & (slot_order[:, :, :, None] == jnp.arange(slots, dtype=jnp.int32))
    ).astype(jnp.int32)
    slot_head = jnp.sum(picked * local_head[:, None, :, None], axis=2)
    slot_gate = jnp.sum(picked * gate_fixed[:, None, :, None], axis=2)
    member = jnp.any(in_group, axis=2).astype(jnp.int32)
    ranking = jnp.cumsum(member, axis=0) - 1
    retained = (member > 0) & (ranking < capacity)
    selected = (
        retained[:, :, None] & (ranking[:, :, None] == jnp.arange(capacity, dtype=jnp.int32))
    ).astype(jnp.int32)
    return (selected, slot_head, slot_gate)


MESH = pl.DeviceIdType.MESH
KV, WQ, WO = 0, 1, 2


def kernel(
    nz, nx, ng, group_heads, slots,
    kv_in, wq_in, wo_in, tokens_ref, sel_ref, meta_in,
    out_ref,
    rows, kvs, wq, wo, q_all, queries, acc, top, total, weighted, contrib, back,
    local_sem, row_send, row_recv, kv_send, kv_recv, gather_send, gather_recv, back_send, back_recv,
    half_send, half_recv, rows_in, meta, meta_send, meta_recv, sel_t,
):
    nb = nz * nx
    s, g = lax.axis_index("seq"), lax.axis_index("grp")
    z, x = s // nx, s % nx
    _, cap, width = rows.shape
    slot_rows = ng * cap
    depth = wq.shape[1]
    out_cols = wo.shape[2]
    tok = kvs.shape[2]
    keys = ng * tok
    hd = kvs.shape[3] // 2
    bufs = (kvs, wq, wo)

    def xs(k):
        return (z * nx + (x + k) % nx, g)

    def peer(k):
        return (g + k) % ng

    barrier = pltpu.get_barrier_semaphore()

    def greet(dev):
        pl.semaphore_signal(barrier, inc=1, device_id=dev, device_id_type=MESH)

    for k in range(1, nx):
        greet(xs(k))
    for k in range(1, ng):
        greet((s, peer(k)))

    @pl.when(z > 0)
    def _():
        greet((s - nx, g))

    @pl.when(z < nz - 1)
    def _():
        greet((s + nx, g))

    peers = nx - 1 + ng - 1 + (z > 0).astype(jnp.int32) + (z < nz - 1).astype(jnp.int32)
    pl.semaphore_wait(barrier, peers)

    own = [
        pltpu.make_async_copy(wq_in, wq.at[s], local_sem.at[0]),
        pltpu.make_async_copy(kv_in.at[g], kvs.at[s, g], local_sem.at[1]),
        pltpu.make_async_copy(wo_in, wo.at[s], local_sem.at[2]),
    ]
    for copy in own:
        copy.start()

    def kv_copy(k):
        to = peer(k)
        return pltpu.make_async_remote_copy(
            kv_in.at[to], kvs.at[s, g], kv_send.at[k - 1], kv_recv.at[k - 1], (s, to), MESH
        )

    def kv_arrival(k):
        frm = peer(ng - k)
        return pltpu.make_async_remote_copy(
            kv_in.at[g], kvs.at[s, frm], kv_send.at[k - 1], kv_recv.at[k - 1], (s, frm), MESH
        )

    def meta_copy(k):
        to = peer(k)
        return pltpu.make_async_remote_copy(
            meta_in.at[to], meta.at[g], meta_send.at[k - 1], meta_recv.at[k - 1], (s, to), MESH
        )

    def meta_arrival(k):
        frm = peer(ng - k)
        return pltpu.make_async_remote_copy(
            meta_in.at[g], meta.at[frm], meta_send.at[k - 1], meta_recv.at[k - 1], (s, frm), MESH
        )

    def row_copy(k):
        to = peer(k)
        return pltpu.make_async_remote_copy(
            rows_in.at[to], rows.at[g], row_send.at[k - 1], row_recv.at[k - 1], (s, to), MESH
        )

    def row_arrival(k):
        frm = peer(ng - k)
        return pltpu.make_async_remote_copy(
            rows_in.at[g], rows.at[frm], row_send.at[k - 1], row_recv.at[k - 1], (s, frm), MESH
        )

    def part(t, b, which):
        if which is None:
            return bufs[t].at[b]
        rows_half = bufs[t].shape[1] // 2
        return bufs[t].at[b, which * rows_half : (which + 1) * rows_half]

    def is_end(zz):
        return (zz == 0) | (zz == nz - 1)

    def gather(t, zz, kind, dev, which=None):
        here = part(t, zz * nx + x, which)
        return pltpu.make_async_remote_copy(
            here, here,
            gather_send.at[(t * nz + zz) * (nx + 1) + kind],
            gather_recv.at[t * nb + zz * nx + x], dev, MESH,
        )

    def arrival(t, b, which=None):
        here = part(t, b, which)
        return pltpu.make_async_remote_copy(
            here, here, gather_send.at[0], gather_recv.at[t * nb + b], (s, peer(1)), MESH
        )

    def half(t, way, k):
        end = 0 if way == 0 else nz - 1
        here = part(t, end * nx + (x + k) % nx, 1)
        at = (t * 2 + way) * nx + k
        to = s + nx if way == 0 else s - nx
        return pltpu.make_async_remote_copy(
            here, here, half_send.at[at], half_recv.at[at], (to, g), MESH
        )

    def half_arrival(t, way, k):
        end = 0 if way == 0 else nz - 1
        here = part(t, end * nx + (x + k) % nx, 1)
        at = (t * 2 + way) * nx + k
        return pltpu.make_async_remote_copy(
            here, here, half_send.at[at], half_recv.at[at], (s, peer(1)), MESH
        )

    def up(t, zz):
        @pl.when(z < nz - 1)
        def _():
            gather(t, zz, 0, (s + nx, g)).start()

    def down(t, zz):
        @pl.when(z > 0)
        def _():
            gather(t, zz, 1, (s - nx, g)).start()

    def send_own(t):
        up(t, z)
        down(t, z)
        for k in range(1, nx):
            gather(t, z, 1 + k, xs(k)).start()

    def across(t, zz):
        @pl.when(is_end(zz))
        def _():
            for k in range(1, nx):
                gather(t, zz, 1 + k, xs(k), 0).start()

        @pl.when(jnp.logical_not(is_end(zz)))
        def _():
            for k in range(1, nx):
                gather(t, zz, 1 + k, xs(k)).start()

    def column_stage(t, d):
        @pl.when(z - d >= 0)
        def _():
            arrival(t, (z - d) * nx + x).wait_recv()
            up(t, z - d)
            across(t, z - d)

        @pl.when(z + d < nz)
        def _():
            arrival(t, (z + d) * nx + x).wait_recv()
            down(t, z + d)
            across(t, z + d)

    def half_stage(t, e):
        for way in (0, 1):
            @pl.when(z == (e if way == 0 else nz - 1 - e))
            def _():
                for k in range(1, nx):
                    if e == 0:
                        arrival(t, z * nx + (x + k) % nx).wait_recv()
                    else:
                        half_arrival(t, way, k).wait_recv()
                    half(t, way, k).start()

    def stage(t, d):
        column_stage(t, d)
        if d == 1:
            half_stage(t, 0)
        if d < nz - 1:
            half_stage(t, d)

    def consume(t, zz, k):
        b = zz * nx + (x + k) % nx

        @pl.when((zz == z) & jnp.logical_not(is_end(z)))
        def _():
            arrival(t, b).wait_recv()

        @pl.when((zz != z) & jnp.logical_not(is_end(zz)))
        def _():
            arrival(t, b).wait_recv()

        @pl.when((zz != z) & is_end(zz))
        def _():
            arrival(t, b, 0).wait_recv()

        @pl.when((zz == 0) & (z == nz - 1))
        def _():
            half_arrival(t, 0, k).wait_recv()

        @pl.when((zz == nz - 1) & (z == 0))
        def _():
            half_arrival(t, 1, k).wait_recv()

    for k in range(1, ng):
        kv_copy(k).start()
    own[0].wait()
    send_own(WQ)
    for k in range(1, ng):
        meta_copy(k).start()
    own[1].wait()
    for k in range(1, ng):
        kv_arrival(k).wait_recv()
    send_own(KV)

    def pick(i, carry):
        cols = pl.ds(pl.multiple_of(i * 512, 128), 512)
        piece = jnp.dot(sel_ref[...], tokens_ref[:, cols], preferred_element_type=jnp.float32)
        rows_in[:, :, cols] = piece.astype(jnp.bfloat16).reshape(ng, cap, 512)
        return carry

    lax.fori_loop(0, width // 512, pick, 0)
    for k in range(1, ng):
        row_copy(k).start()
    rows[g] = rows_in[g]
    meta[g] = meta_in[g]
    sel_t[...] = sel_ref[...].astype(jnp.float32).T.astype(jnp.bfloat16)
    own[2].wait()
    for d in range(1, nz):
        stage(KV, d)
        stage(WQ, d)
        if d == 1:
            send_own(WO)
        if d == max(nz - 2, 1):
            column_stage(WO, 1)
    half_stage(WO, 0)
    if nz > 2:
        half_stage(WO, 1)

    for k in range(1, ng):
        row_arrival(k).wait_recv()
        meta_arrival(k).wait_recv()

    def shard_at(i):
        return jnp.where(z * 2 < nz, i % nz, nz - 1 - i % nz)

    def block_at(i):
        return shard_at(i) * nx + (x + i // nz) % nx

    def consume_from(t, i):
        for k in range(1, nx):
            @pl.when(i // nz == k)
            def _():
                consume(t, shard_at(i), k)

    q_all[...] = jnp.zeros_like(q_all)

    def project(i, carry):
        b = block_at(i)

        consume_from(WQ, i)

        piece = rows[:, :, pl.ds(pl.multiple_of(b * depth, 128), depth)].reshape(slot_rows, depth)
        q_all[...] += jnp.dot(piece, wq[b], preferred_element_type=jnp.float32)
        return carry

    lax.fori_loop(0, nb, project, 0)

    def meta_column(i):
        return meta[:, :, i : i + 1].reshape(slot_rows, 1)

    for j in range(slots):
        head = meta_column(j)
        q = jnp.zeros((slot_rows, hd), jnp.float32)
        for h in range(group_heads):
            q = jnp.where(head == h, q_all[:, h * hd : (h + 1) * hd], q)
        queries[j] = q.astype(jnp.bfloat16)

    for k in range(1, nx):
        for zz in range(nz):
            consume(KV, zz, k)

    def update(j, b, masked):
        k = kvs[b, :, :, :hd].reshape(keys, hd)
        v = kvs[b, :, :, hd:].reshape(keys, hd)
        scores = lax.dot_general(
            queries[j], k, (((1,), (1,)), ((), ())), preferred_element_type=jnp.float32
        ) * (hd ** -0.5)
        if masked:
            key_pos = b * keys + lax.broadcasted_iota(jnp.int32, scores.shape, 1)
            scores = jnp.where(key_pos <= meta_column(2 * slots), scores, -1e30)
        before = top[...]
        newest = jnp.maximum(before, jnp.max(scores, axis=1, keepdims=True))
        weights = jnp.exp(scores - newest)
        factor = jnp.exp(before - newest)
        total[...] = total[...] * factor + jnp.sum(weights, axis=1, keepdims=True)
        acc[j] = acc[j] * factor + jnp.dot(
            weights.astype(jnp.bfloat16), v, preferred_element_type=jnp.float32
        )
        top[...] = newest

    def attend(j):
        top[...] = jnp.full_like(top, -1e30)
        total[...] = jnp.zeros_like(total)
        acc[j] = jnp.zeros((slot_rows, hd), jnp.float32)

        def step(b, carry):
            update(j, b, False)
            return carry

        lax.fori_loop(0, s, step, 0)
        update(j, s, True)
        acc[j] = acc[j] / total[...] * (meta_column(slots + j).astype(jnp.float32) / 32768.0)

    def rest(last):
        for d in range(2, last + 1):
            stage(WO, d)

    @pl.when(jnp.logical_not(is_end(z)))
    def _():
        rest(nz - 2)

    for n in range(slots):
        if n == slots - 1:
            @pl.when(is_end(z))
            def _():
                rest(nz - 2)

        attend(n)
    if nz > 2:
        stage(WO, nz - 1)

    for h in range(group_heads):
        value = jnp.zeros((slot_rows, hd), jnp.float32)
        for j in range(slots):
            value += jnp.where(meta_column(j) == h, acc[j], 0.0)
        weighted[:, h * hd : (h + 1) * hd] = value.astype(jnp.bfloat16)

    def back_copy(b, k):
        to = peer(k)
        return pltpu.make_async_remote_copy(
            contrib.at[b, to], back.at[b, g],
            back_send.at[b * (ng - 1) + k - 1], back_recv.at[b * (ng - 1) + k - 1], (s, to), MESH,
        )

    def back_arrival(b, k):
        frm = peer(ng - k)
        return pltpu.make_async_remote_copy(
            contrib.at[b, g], back.at[b, frm],
            back_send.at[b * (ng - 1) + k - 1], back_recv.at[b * (ng - 1) + k - 1], (s, frm), MESH,
        )

    def give_back(i, carry):
        b = block_at(i)

        consume_from(WO, i)

        product = jnp.dot(weighted[...], wo[b], preferred_element_type=jnp.float32)
        contrib[b] = product.astype(jnp.bfloat16).reshape(ng, cap, out_cols)
        for k in range(1, ng):
            back_copy(b, k).start()
        back[b, g] = contrib[b, g]
        return carry

    lax.fori_loop(0, nb, give_back, 0)

    def combine(i, carry):
        b = block_at(i)
        for k in range(1, ng):
            back_arrival(b, k).wait_recv()
        mixed = jnp.dot(
            sel_t[...], back[b].reshape(slot_rows, out_cols), preferred_element_type=jnp.float32
        )
        out_ref[:, pl.ds(pl.multiple_of(b * out_cols, 128), out_cols)] = mixed.astype(jnp.bfloat16)
        for k in range(1, ng):
            back_copy(b, k).wait_send()
        return carry

    lax.fori_loop(0, nb, combine, 0)

    for k in range(1, ng):
        kv_copy(k).wait_send()
        row_copy(k).wait_send()
        meta_copy(k).wait_send()
    for t in (KV, WQ, WO):
        for zz in range(nz):
            @pl.when((zz <= z) & (z < nz - 1))
            def _():
                gather(t, zz, 0, (s + nx, g)).wait_send()

            @pl.when((zz >= z) & (z > 0))
            def _():
                gather(t, zz, 1, (s - nx, g)).wait_send()

            if zz in (0, nz - 1):
                for k in range(1, nx):
                    @pl.when(z == zz)
                    def _():
                        gather(t, zz, 1 + k, xs(k)).wait_send()

                    @pl.when(z != zz)
                    def _():
                        gather(t, zz, 1 + k, xs(k), 0).wait_send()
            else:
                for k in range(1, nx):
                    gather(t, zz, 1 + k, xs(k)).wait_send()

        for k in range(1, nx):
            @pl.when(z < nz - 1)
            def _():
                half(t, 0, k).wait_send()

            @pl.when(z > 0)
            def _():
                half(t, 1, k).wait_send()


def on_device(nz, tokens, head_index, gate_fixed, kv_weight, query_weight, out_weight):
    groups = lax.axis_size("grp")
    nb = lax.axis_size("seq")
    nx = nb // nz
    tok_rows, model_width = tokens.shape
    capacity = 3 * tok_rows // groups
    head_width = kv_weight.shape[2] // 2
    group_heads = query_weight.shape[1] // head_width
    slots = head_index.shape[1] - 1
    offset = (lax.axis_index("seq") * groups + lax.axis_index("grp")) * tok_rows
    positions = offset + jnp.arange(tok_rows, dtype=jnp.int32)
    kv_local = jnp.einsum(
        "td,dgc->gtc", tokens, kv_weight, preferred_element_type=jnp.float32
    ).astype(jnp.bfloat16)
    selected, slot_head, slot_gate = route_tables(
        head_index, gate_fixed, groups, capacity, group_heads
    )
    by_slot = jnp.transpose(selected, (1, 2, 0))
    send_pos = jnp.sum(by_slot * positions[None, None, :], axis=2)
    send_head = jnp.sum(
        by_slot[:, :, :, None] * jnp.transpose(slot_head, (1, 0, 2))[:, None, :, :], axis=2
    )
    send_gate = jnp.sum(
        by_slot[:, :, :, None] * jnp.transpose(slot_gate, (1, 0, 2))[:, None, :, :], axis=2
    )
    send_meta = jnp.concatenate([send_head, send_gate, send_pos[:, :, None]], axis=2)
    send_meta = jnp.pad(send_meta, ((0, 0), (0, 0), (0, 128 - send_meta.shape[2])))
    slot_rows = groups * capacity
    sel = by_slot.astype(jnp.bfloat16).reshape(slot_rows, tok_rows)
    bf, f32 = jnp.bfloat16, jnp.float32
    depth, q_cols = query_weight.shape
    out_cols = out_weight.shape[1]
    any_spec = pl.BlockSpec(memory_space=pl.ANY)
    vmem_spec = pl.BlockSpec(memory_space=pltpu.VMEM)
    dma = pltpu.SemaphoreType.DMA
    return pl.pallas_call(
        functools.partial(kernel, nz, nx, groups, group_heads, slots),
        out_shape=jax.ShapeDtypeStruct((tok_rows, model_width), bf),
        in_specs=[any_spec] * 3 + [vmem_spec] * 3,
        out_specs=vmem_spec,
        scratch_shapes=[
            pltpu.VMEM((groups, capacity, model_width), bf),
            pltpu.VMEM((nb, groups, tok_rows, 2 * head_width), bf),
            pltpu.VMEM((nb, depth, q_cols), bf),
            pltpu.VMEM((nb, q_cols, out_cols), bf),
            pltpu.VMEM((slot_rows, q_cols), f32),
            pltpu.VMEM((slots, slot_rows, head_width), bf),
            pltpu.VMEM((slots, slot_rows, head_width), f32),
            pltpu.VMEM((slot_rows, 1), f32),
            pltpu.VMEM((slot_rows, 1), f32),
            pltpu.VMEM((slot_rows, q_cols), bf),
            pltpu.VMEM((nb, groups, capacity, out_cols), bf),
            pltpu.VMEM((nb, groups, capacity, out_cols), bf),
            dma((3,)),
            dma((groups - 1,)),
            dma((groups - 1,)),
            dma((groups - 1,)),
            dma((groups - 1,)),
            dma((3 * nz * (nx + 1),)),
            dma((3 * nb,)),
            dma((nb * (groups - 1),)),
            dma((nb * (groups - 1),)),
            dma((3 * 2 * nx,)),
            dma((3 * 2 * nx,)),
            pltpu.VMEM((groups, capacity, model_width), bf),
            pltpu.VMEM((groups, capacity, 128), jnp.int32),
            dma((groups - 1,)),
            dma((groups - 1,)),
            pltpu.VMEM((tok_rows, slot_rows), bf),
        ],
        compiler_params=pltpu.CompilerParams(
            collective_id=0, has_side_effects=True, vmem_limit_bytes=56 * 2**20
        ),
    )(kv_local, query_weight, out_weight, tokens, sel, send_meta)


def solution(mesh):
    in_specs = (
        P(("seq", "grp"), None),
        P(("seq", "grp"), None),
        P(("seq", "grp"), None),
        P(),
        P("seq", "grp"),
        P("grp", "seq"),
    )
    out_specs = P(("seq", "grp"), None)
    nz = 4 if mesh.shape["seq"] % 4 == 0 else mesh.shape["seq"]
    return jax.shard_map(
        functools.partial(on_device, nz),
        mesh=mesh, in_specs=in_specs, out_specs=out_specs, check_vma=False,
    )
```
